256 devices in a mesh: dp: 8 (over x, z_lo), expert: 32 (over y, z_hi, core).
Axes of the slice: x: 4, y: 4, z: 8 (z_hi: 4, z_lo: 2; z = z_hi * 2 + z_lo), core: 2. Of those that a mesh axis runs over, the one named last changes fastest.
Arguments:
- tokens: bfloat16 [32768, 1664], P(('dp', 'expert')), may hold values from -6 to 6
- cotangent: bfloat16 [32768, 1664], P(('dp', 'expert')), may hold values from -6 to 6
- expert_idx: int32 [32768, 2], P(('dp', 'expert')), may hold values from 0 to 31, as said below
- expert_slot: int32 [32768, 2], P(('dp', 'expert')), may hold values from -1 to 5, as said below
- combine: float32 [32768, 2], P(('dp', 'expert')), may hold values from 0.2 to 1
- gain: float32 [1664], replicated, may hold values from 0.5 to 1.5
- shift: float32 [1664], replicated, may hold values from -3 to 3
- w_in: bfloat16 [32, 1664, 4096], P('expert', None, 'dp'), may hold values from -0.15625 to 0.15625
- b_in: float32 [32, 4096], P('expert', 'dp'), may hold values from -3 to 3
- w_out: bfloat16 [32, 4096, 1664], P('expert', 'dp'), may hold values from -0.09375 to 0.09375
Outputs:
- grad_tokens: bfloat16 [32768, 1664], P(('dp', 'expert'))
- grad_w_in: float32 [32, 1664, 4096], P('expert', None, 'dp')
- grad_b_in: float32 [32, 4096], P('expert', 'dp')
- grad_w_out: float32 [32, 4096, 1664], P('expert', 'dp')
- gain_gradient: float32 [1664], replicated
- grad_shift: float32 [1664], replicated
The draws below stay inside these ranges and needn't reach their ends.
Inputs may be any that keep to these rules, and one draw needn't show every extreme that they name: `expert_idx`: an expert number of 0 to 31; the two choices of a patch differ. `expert_slot`: within the 128 patches of one device, the live slots of one expert are 0, 1, ... without repeats, at most 6 of them; -1 marks a dropped choice.
All inputs are finite; a program needn't handle non-finite values.
Results may differ from the reference program's by a relative error of at most 0.018.
Values may be sent and summed in bfloat16 or wider, within the bound.
No kernel may reach another device: no remote copies, remote signals or barrier semaphores. Data moves between devices by JAX's collectives and lax.ppermute only.
A program may use at most 128 MiB of HBM per device.

```python
import math
import jax
import jax.numpy as jnp
from jax import lax

D = 1664
H = 4096
TOP = 2
TOK_DEV = 128
EXPERTS = 32
CAP = 6
TOKENS = 32768
N_DP = 8


def routing_tables(key):
    nblocks = TOKENS // TOK_DEV
    key_a, key_b, key_c, key_d = jax.random.split(key, 4)
    first_raw = jax.random.randint(key_a, (nblocks, TOK_DEV), 0, EXPERTS)
    second_raw = jax.random.randint(key_b, (nblocks, TOK_DEV), 0, EXPERTS)
    skewed = first_raw * second_raw // EXPERTS
    order = jax.random.permutation(key_c, EXPERTS)
    first = order[skewed]
    local = jnp.arange(TOK_DEV, dtype=jnp.int32)[None, :]
    first = jnp.where(local <= CAP, order[0], first)
    offset = jax.random.randint(key_d, (nblocks, TOK_DEV), 1, EXPERTS)
    second = (first + offset) % EXPERTS
    picks = jnp.stack([first, second], axis=1).reshape(nblocks, 2 * TOK_DEV)
    onehot = (picks[:, :, None] == jnp.arange(EXPERTS, dtype=jnp.int32)[None, None, :]).astype(jnp.int32)
    before = jnp.cumsum(onehot, axis=1) - onehot
    rank = jnp.sum(before * onehot, axis=-1)
    slots = jnp.where(rank < CAP, rank, -1)
    picks = jnp.transpose(picks.reshape(nblocks, 2, TOK_DEV), (0, 2, 1)).reshape(TOKENS, 2)
    slots = jnp.transpose(slots.reshape(nblocks, 2, TOK_DEV), (0, 2, 1)).reshape(TOKENS, 2)
    return (picks.astype(jnp.int32), slots.astype(jnp.int32))


def draw_expert_idx(key, part):
    picks, slots = routing_tables(key)
    return picks


def draw_expert_slot(key, part):
    picks, slots = routing_tables(key)
    return slots


def shard_levels(key, dims, pieces, least, largest):
    level = 1.0
    for position, blocks in pieces:
        heights = jax.random.uniform(jax.random.fold_in(jax.random.fold_in(key, 6), position), (blocks,), jnp.float32, least / len(pieces), largest / len(pieces))
        level = level * jnp.repeat(jnp.exp(heights), dims[position] // blocks).reshape((-1,) + (1,) * (len(dims) - 1 - position))
    return level


def scatter_about(own_key, shape, scale, bound, shards=(), kind=jnp.bfloat16):
    drawn = jax.random.normal(own_key, shape, jnp.float32) * scale
    if len(shards) > 0:
        drawn = shard_levels(own_key, shape, shards, -0.22, 0.18) * drawn
    return jnp.clip(drawn, min=-bound, max=bound).astype(kind)


def setup_inputs(seed: int = 0) -> dict:
    keys = jax.random.split(jax.random.key(seed), 11)
    return {
        "tokens": scatter_about(keys[0], (TOKENS, D), 1.0, 6.0, ((0, 256),)),
        "cotangent": scatter_about(keys[1], (TOKENS, D), 1.0, 6.0, ((0, 256),)),
        "expert_idx": draw_expert_idx(jax.random.fold_in(keys[10], 71), 0),
        "expert_slot": draw_expert_slot(jax.random.fold_in(keys[10], 71), 0),
        "combine": jnp.clip(0.2 + 0.8 * jax.random.uniform(keys[4], (TOKENS, TOP), jnp.float32) ** shard_levels(keys[4], (TOKENS, TOP), ((0, 256),), -0.2, 0.2), 0.2, 1.0),
        "gain": jnp.clip(1.0 + 0.1 * jax.random.normal(keys[5], (D,), jnp.float32), 0.5, 1.5),
        "shift": scatter_about(keys[6], (D,), 0.5, 3.0, (), jnp.float32),
        "w_in": scatter_about(keys[7], (EXPERTS, D, H), D ** -0.5, 0.15625, ((0, 32), (2, 8))),
        "b_in": scatter_about(keys[8], (EXPERTS, H), 0.5, 3.0, ((0, 32), (1, 8)), jnp.float32),
        "w_out": scatter_about(keys[9], (EXPERTS, H, D), H ** -0.5, 0.09375, ((0, 32), (1, 8))),
    }


inv_root_two = 1.0 / math.sqrt(2.0)
inv_root_tau = 1.0 / math.sqrt(2.0 * math.pi)

def gelu_parts(value):
    normal_cdf = 0.5 * (1.0 + jax.scipy.special.erf(value * inv_root_two))
    slope = normal_cdf + value * jnp.exp(-0.5 * value * value) * inv_root_tau
    return (value * normal_cdf, slope)

def reference(tokens, cotangent, expert_idx, expert_slot, combine, gain, shift, w_in, b_in, w_out):
    floats = tokens.astype(jnp.float32)
    centered_rows = floats - lax.optimization_barrier(jnp.mean(floats, axis=-1, keepdims=True))
    inverse_deviation = lax.rsqrt(lax.optimization_barrier(jnp.mean(centered_rows * centered_rows, axis=-1, keepdims=True)) + 1e-06)
    standardized_input = centered_rows * inverse_deviation
    normalized_rows = (standardized_input * gain + shift).astype(jnp.bfloat16)
    nblocks = TOKENS // TOK_DEV
    block = (jnp.arange(TOKENS) // TOK_DEV).astype(jnp.int32)
    live = expert_slot >= 0
    dest_e = jnp.where(live, expert_idx, EXPERTS).astype(jnp.int32)
    dest_s = jnp.where(live, expert_slot, 0).astype(jnp.int32)
    rows_in = jnp.zeros((EXPERTS, nblocks, CAP, D), jnp.bfloat16)
    rows_grad = jnp.zeros((EXPERTS, nblocks, CAP, D), jnp.bfloat16)
    grad_f = cotangent.astype(jnp.float32)
    for choice_k in range(TOP):
        scaled = (combine[:, choice_k:choice_k + 1] * grad_f).astype(jnp.bfloat16)
        rows_in = rows_in.at[dest_e[:, choice_k], block, dest_s[:, choice_k]].set(normalized_rows, mode='drop')
        rows_grad = rows_grad.at[dest_e[:, choice_k], block, dest_s[:, choice_k]].set(scaled, mode='drop')
    width = H // N_DP
    count = nblocks * CAP

    def per_expert(operands):
        weight_in, bias_in, weight_out, inputs, grads = operands
        inputs = inputs.reshape(count, D)
        grads = grads.reshape(count, D)
        pre = jnp.dot(inputs, weight_in, preferred_element_type=jnp.float32) + bias_in
        act_value, slope = gelu_parts(pre)
        act = act_value.astype(jnp.bfloat16)
        grad_wout = jnp.dot(act.T, grads, preferred_element_type=jnp.float32)
        grad_act = jnp.dot(grads, weight_out.T, preferred_element_type=jnp.float32)
        grad_pre = grad_act * slope
        grad_bias = lax.optimization_barrier(jnp.sum(grad_pre, axis=0))
        grad_pre_b = grad_pre.astype(jnp.bfloat16)
        grad_win = jnp.dot(inputs.T, grad_pre_b, preferred_element_type=jnp.float32)
        partial_rows = jnp.einsum('rph,dph->prd', grad_pre_b.reshape(count, N_DP, width).astype(jnp.float32), weight_in.reshape(D, N_DP, width).astype(jnp.float32), precision=lax.Precision.HIGHEST)
        rounded = lax.optimization_barrier(partial_rows.astype(jnp.bfloat16))
        back = lax.optimization_barrier(jnp.sum(rounded.astype(jnp.float32), axis=0)).astype(jnp.bfloat16)
        return (grad_win, grad_bias, grad_wout, back.reshape(nblocks, CAP, D))
    grad_w_in, grad_b_in, grad_w_out, grad_rows = lax.map(per_expert, (w_in, b_in, w_out, rows_in, rows_grad))
    normalized_gradient = jnp.zeros((TOKENS, D), jnp.float32)
    for choice_k in range(TOP):
        picked = grad_rows[jnp.minimum(dest_e[:, choice_k], EXPERTS - 1), block, dest_s[:, choice_k]]
        normalized_gradient = normalized_gradient + jnp.where(live[:, choice_k:choice_k + 1], picked.astype(jnp.float32), 0.0)
    gain_gradient = lax.optimization_barrier(jnp.sum(normalized_gradient * standardized_input, axis=0))
    grad_shift = lax.optimization_barrier(jnp.sum(normalized_gradient, axis=0))
    gain_scaled_gradient = normalized_gradient * gain
    inner_product = gain_scaled_gradient - lax.optimization_barrier(jnp.mean(gain_scaled_gradient, axis=-1, keepdims=True)) - standardized_input * lax.optimization_barrier(jnp.mean(gain_scaled_gradient * standardized_input, axis=-1, keepdims=True))
    grad_tokens = (grad_f + inverse_deviation * inner_product).astype(jnp.bfloat16)
    return (grad_tokens, grad_w_in, grad_b_in, grad_w_out, gain_gradient, grad_shift)
```

```python
import math

import jax
import jax.numpy as jnp
from jax import lax
from jax.sharding import PartitionSpec as P

inv_root_two = 1.0 / math.sqrt(2.0)
inv_root_tau = 1.0 / math.sqrt(2.0 * math.pi)

RIGHT = [(i, (i + 2) % 8) for i in range(8)]
LEFT = [(i, (i - 2) % 8) for i in range(8)]
ACROSS = [(i, i ^ 1) for i in range(8)]


def gelu_parts(value):
    normal_cdf = 0.5 * (1.0 + jax.scipy.special.erf(value * inv_root_two))
    slope = normal_cdf + value * jnp.exp(-0.5 * value * value) * inv_root_tau
    return (value * normal_cdf, slope)


def right(x):
    return lax.ppermute(x, "dp", RIGHT)


def left(x):
    return lax.ppermute(x, "dp", LEFT)


def across(x):
    return lax.ppermute(x, "dp", ACROSS)


def swapped(x, mask):
    return lax.ppermute(x, ("dp", "expert"), [(i, i ^ mask) for i in range(256)])


def add16(a, b):
    return (a.astype(jnp.float32) + b.astype(jnp.float32)).astype(jnp.bfloat16)


def total(x):
    x = x + swapped(x, 1)
    for low, high in ((64, 128), (8, 16)):
        x = (x + swapped(x, high)) + (swapped(x, low) + swapped(x, low | high))
    x = x + swapped(x, 32)
    return (x + swapped(x, 4)) + (swapped(x, 2) + swapped(x, 6))


def shards(tokens, cotangent, expert_idx, expert_slot, combine, gain, shift, w_in, b_in, w_out):
    experts = lax.axis_size("expert")
    tok_rows, model_width = tokens.shape
    capacity = max(2, 3 * tok_rows * 2 // (4 * experts))
    floats = tokens.astype(jnp.float32)
    centered_rows = floats - jnp.mean(floats, axis=-1, keepdims=True)
    inverse_deviation = lax.rsqrt(
        jnp.mean(centered_rows * centered_rows, axis=-1, keepdims=True) + 1e-06
    )
    standardized_input = centered_rows * inverse_deviation
    normalized_rows = (standardized_input * gain + shift).astype(jnp.bfloat16)
    codes = jnp.where(expert_slot >= 0, expert_idx * capacity + expert_slot, -1)
    slot_ids = jnp.arange(experts * capacity, dtype=jnp.int32)[:, None]
    select_one = (codes[:, 0][None, :] == slot_ids).astype(jnp.float32)
    select_two = (codes[:, 1][None, :] == slot_ids).astype(jnp.float32)
    dispatch_table = (select_one + select_two).astype(jnp.bfloat16)
    slot_weight = jnp.sum(
        select_one * combine[:, 0][None, :] + select_two * combine[:, 1][None, :], axis=1
    )
    slot_inputs = jnp.dot(
        dispatch_table, normalized_rows, preferred_element_type=jnp.float32
    ).astype(jnp.bfloat16)
    slot_grads = jnp.dot(dispatch_table, cotangent, preferred_element_type=jnp.float32)
    slot_grads = (slot_weight[:, None] * slot_grads).astype(jnp.bfloat16)
    packed = jnp.stack([slot_inputs, slot_grads]).reshape(2, experts, capacity, model_width)
    arrived = lax.all_to_all(packed, "expert", split_axis=1, concat_axis=1, tiled=True)
    rows = experts * capacity
    own_i = arrived[0].reshape(rows, model_width)
    own_g = arrived[1].reshape(rows, model_width)

    weight_in = w_in[0]
    weight_out = w_out[0]

    def forward(inputs, grads):
        pre = jnp.dot(inputs, weight_in, preferred_element_type=jnp.float32) + b_in[0]
        act_value, slope = gelu_parts(pre)
        grad_act = lax.dot_general(
            grads, weight_out, (((1,), (1,)), ((), ())), preferred_element_type=jnp.float32
        )
        grad_pre = grad_act * slope
        grad_pre_b = grad_pre.astype(jnp.bfloat16)
        partial = lax.dot_general(
            grad_pre_b, weight_in, (((1,), (1,)), ((), ())), preferred_element_type=jnp.float32
        ).astype(jnp.bfloat16)
        return act_value.astype(jnp.bfloat16), grad_pre_b, jnp.sum(grad_pre, axis=0), partial

    l_i, r_i, q_i = right(own_i), left(own_i), across(own_i)
    l_g, r_g, q_g = right(own_g), left(own_g), across(own_g)
    ql_i, f_i, qr_i = right(q_i), left(r_i), across(r_i)
    ql_g, f_g, qr_g = right(q_g), left(r_g), across(r_g)
    qf_i = right(ql_i)
    qf_g = left(qr_g)

    cat = lambda *a: jnp.concatenate(a, axis=0)
    in_a, gr_a = cat(own_i, l_i, r_i, q_i), cat(own_g, l_g, r_g, q_g)
    in_b, gr_b = cat(ql_i, f_i, qr_i), cat(ql_g, f_g, qr_g)
    act_a, pre_a, bias_a, part_a = forward(in_a, gr_a)
    act_b, pre_b, bias_b, part_b = forward(in_b, gr_b)
    act_c, pre_c, bias_c, part_c = forward(qf_i, qf_g)
    p_own, p_l, p_r, p_q = jnp.split(part_a, 4)
    p_ql, p_f, p_qr = jnp.split(part_b, 3)
    half = rows // 2
    back_ql = left(part_c[:half])
    back_qr = right(part_c[half:])
    s_ql = cat(add16(p_ql[:half], back_ql), p_ql[half:])
    s_qr = cat(p_qr[:half], add16(p_qr[half:], back_qr))
    s_q = add16(p_q, left(s_ql))
    s_r = (
        p_r.astype(jnp.float32) + right(p_f).astype(jnp.float32) + across(s_qr).astype(jnp.float32)
    ).astype(jnp.bfloat16)
    summed = (
        (p_own.astype(jnp.float32) + left(p_l).astype(jnp.float32))
        + (right(s_r).astype(jnp.float32) + across(s_q).astype(jnp.float32))
    ).astype(jnp.bfloat16)

    inputs = cat(in_a, in_b, qf_i)
    grads = cat(gr_a, gr_b, qf_g)
    act = cat(act_a, act_b, act_c)
    grad_pre_b = cat(pre_a, pre_b, pre_c)
    grad_bias = bias_a + bias_b + bias_c
    grad_win = lax.dot_general(
        inputs, grad_pre_b, (((0,), (0,)), ((), ())), preferred_element_type=jnp.float32
    )
    grad_wout = lax.dot_general(
        act, grads, (((0,), (0,)), ((), ())), preferred_element_type=jnp.float32
    )
    weight_floats = weight_in.astype(jnp.float32)
    sums = total(
        jnp.stack(
            [
                jnp.sum(weight_floats * grad_win, axis=1),
                jnp.sum(weight_floats * grad_bias[None, :], axis=1),
            ]
        )
    )
    grad_shift = sums[1]
    gain_gradient = (sums[0] - shift * grad_shift) / gain

    returned = lax.all_to_all(
        summed.reshape(experts, capacity, model_width), "expert", split_axis=0, concat_axis=0, tiled=True
    )
    back_rows = returned.reshape(rows, model_width)
    normalized_gradient = lax.dot_general(
        dispatch_table, back_rows, (((0,), (0,)), ((), ())), preferred_element_type=jnp.float32
    )
    gain_scaled_gradient = normalized_gradient * gain
    inner_product = (
        gain_scaled_gradient
        - jnp.mean(gain_scaled_gradient, axis=-1, keepdims=True)
        - standardized_input
        * jnp.mean(gain_scaled_gradient * standardized_input, axis=-1, keepdims=True)
    )
    grad_tokens = (cotangent.astype(jnp.float32) + inverse_deviation * inner_product).astype(
        jnp.bfloat16
    )
    return (grad_tokens, grad_win[None], grad_bias[None], grad_wout[None], gain_gradient, grad_shift)


def solution(mesh):
    both = P(("dp", "expert"), None)
    return jax.shard_map(
        shards,
        mesh=mesh,
        in_specs=(both,) * 5
        + (P(), P(), P("expert", None, "dp"), P("expert", "dp"), P("expert", "dp", None)),
        out_specs=(both, P("expert", None, "dp"), P("expert", "dp"), P("expert", "dp", None), P(), P()),
        check_vma=False,
    )
```

```python
import functools
import math

import jax
import jax.numpy as jnp
import numpy as np
from jax import lax
from jax.experimental import pallas as pl
from jax.experimental.pallas import tpu as pltpu
from jax.sharding import PartitionSpec as P

inv_root_two = 1.0 / math.sqrt(2.0)
inv_root_tau = 1.0 / math.sqrt(2.0 * math.pi)
f32, bf16 = jnp.float32, jnp.bfloat16

RIGHT = [(i, (i + 2) % 8) for i in range(8)]
LEFT = [(i, (i - 2) % 8) for i in range(8)]
ACROSS = [(i, i ^ 1) for i in range(8)]
CAP = 6
FIRST, SECOND = pl.ds(0, 896), pl.ds(896, 768)


def gelu_parts(value):
    normal_cdf = 0.5 * (1.0 + lax.erf(value * inv_root_two))
    slope = normal_cdf + value * jnp.exp(-0.5 * value * value) * inv_root_tau
    return (value * normal_cdf, slope)


def right(x):
    return lax.ppermute(x, "dp", RIGHT)


def left(x):
    return lax.ppermute(x, "dp", LEFT)


def across(x):
    return lax.ppermute(x, "dp", ACROSS)


def swapped(x, mask):
    return lax.ppermute(x, ("dp", "expert"), [(i, i ^ mask) for i in range(256)])


def add16(*terms):
    total = terms[0].astype(f32)
    for term in terms[1:]:
        total = total + term.astype(f32)
    return total.astype(bf16)


def chip_exchange(x):
    groups = [[2 * n + core for n in range(16)] for core in (0, 1)]
    x = x.reshape(16, x.shape[0] // 16, x.shape[1])
    x = lax.all_to_all(x, "expert", 0, 0, axis_index_groups=groups, tiled=True)
    return x.reshape(-1, x.shape[2])


def layer_norm(tokens):
    floats = tokens.astype(f32)
    centered = floats - jnp.mean(floats, axis=-1, keepdims=True)
    deviation = lax.rsqrt(jnp.mean(centered * centered, axis=-1, keepdims=True) + 1e-06)
    return centered * deviation, deviation


def dispatch_kernel(tok, cot, idx, slot, comb, gain, shift, near, far, both):
    standardized, _ = layer_norm(tok[...])
    both[:128, :] = (standardized * gain[...] + shift[...]).astype(bf16)
    both[128:, :] = cot[...]
    expert = idx[...]
    core = (expert ^ lax.axis_index("expert")) & 1
    code = jnp.where(slot[...] >= 0, core * 192 + (expert >> 1) * 12 + slot[...], -1000)
    for part, out in enumerate((near, far)):
        row = lax.broadcasted_iota(jnp.int32, (192, 128), 0) + part * 192
        ins = [(code[k : k + 1, :] == row).astype(f32) for k in (0, 1)]
        outs = [(code[k : k + 1, :] + CAP == row).astype(f32) for k in (0, 1)]
        scale = jnp.sum(
            ins[0] + ins[1] + outs[0] * comb[0:1, :] + outs[1] * comb[1:2, :], axis=1, keepdims=True
        )
        table = jnp.concatenate([ins[0] + ins[1], outs[0] + outs[1]], axis=1).astype(bf16)
        picked = jnp.dot(table, both[...], preferred_element_type=f32)
        out[...] = (picked * scale).astype(bf16)


def regroup_kernel(count, table, *refs):
    ins, outs, buffer = refs[:count], refs[count:-1], refs[-1]
    size = ins[0].shape[0]
    for n, ref in enumerate(ins):
        buffer[n * size : (n + 1) * size, :] = ref[...]
    start = 0
    for out in outs:
        columns = out.shape[1]
        out[...] = jnp.dot(
            table[...], buffer[:, start : start + columns], preferred_element_type=f32
        ).astype(bf16)
        start += columns


def regroup(order, pieces, widths):
    rows, width = pieces[0].shape
    whole = rows * len(pieces)
    table = jnp.asarray(order[:, None] == np.arange(whole)[None, :], bf16)
    return pl.pallas_call(
        functools.partial(regroup_kernel, len(pieces)),
        out_shape=[jax.ShapeDtypeStruct((whole, n), bf16) for n in widths],
        scratch_shapes=[pltpu.VMEM((whole, width), bf16)],
        compiler_params=pltpu.CompilerParams(vmem_limit_bytes=24 * 2**20),
        cost_estimate=pl.CostEstimate(flops=1, bytes_accessed=1, transcendentals=0),
    )(table, *pieces)


def experts_kernel(blocks, place, aliased, weight_in, in_turned, out_turned, bias_in, *refs):
    firsts, seconds = refs[:blocks], refs[blocks : 2 * blocks]
    refs = refs[2 * blocks + 4 * aliased :]
    all_in, all_gr, all_act, all_pre, bias = refs[:5]
    partials, (inputs, grads, act, grad_pre, sems, out_sems) = refs[5:-6], refs[-6:]
    rows = 192 * blocks
    copies = []
    for b in range(blocks):
        r = pl.ds(192 * b, 192)
        for n, (kind, whole) in enumerate(((pl.ds(0, 192), inputs), (pl.ds(192, 192), grads))):
            for m, (part, columns) in enumerate(((firsts[b], FIRST), (seconds[b], SECOND))):
                sem = sems.at[4 * b + 2 * n + m]
                copies.append(pltpu.make_async_copy(part.at[kind], whole.at[r, columns], sem))
    for copy in copies:
        copy.start()
    for copy in copies:
        copy.wait()
    there = pl.ds(place, rows)
    keep = [
        pltpu.make_async_copy(here, out.at[there], out_sems.at[n])
        for n, (here, out) in enumerate(
            [(inputs, all_in), (grads, all_gr), (act, all_act), (grad_pre, all_pre)]
        )
    ]
    keep[0].start()
    keep[1].start()
    pre = jnp.dot(inputs[...], weight_in[...], preferred_element_type=f32) + bias_in[...]
    act_value, slope = gelu_parts(pre)
    act[...] = act_value.astype(bf16)
    keep[2].start()
    grad = slope * jnp.dot(grads[...], out_turned[...], preferred_element_type=f32)
    bias[...] = jnp.sum(grad, axis=0, keepdims=True)
    grad_pre[...] = grad.astype(bf16)
    keep[3].start()
    partial = jnp.dot(grad_pre[...], in_turned[...], preferred_element_type=f32).astype(bf16)
    start = 0
    for out in partials:
        out[...] = partial[start : start + out.shape[0], :]
        start += out.shape[0]
    for copy in keep:
        copy.wait()


def experts_step(weights, bias_in, place, blocks, kept, sizes):
    rows = 192 * len(blocks)
    width = weights[0].shape[0]
    vmem, anywhere = pl.BlockSpec(memory_space=pltpu.VMEM), pl.BlockSpec(memory_space=pl.ANY)
    first = 4 + 2 * len(blocks)
    out = pl.pallas_call(
        functools.partial(experts_kernel, len(blocks), place, kept is not None),
        in_specs=[vmem] * 4 + [anywhere] * (2 * len(blocks) + (4 if kept else 0)),
        out_specs=[anywhere] * 4 + [vmem] * (1 + len(sizes)),
        out_shape=[
            jax.ShapeDtypeStruct((1536, width), bf16),
            jax.ShapeDtypeStruct((1536, width), bf16),
            jax.ShapeDtypeStruct((1536, 512), bf16),
            jax.ShapeDtypeStruct((1536, 512), bf16),
            jax.ShapeDtypeStruct((1, 512), f32),
        ]
        + [jax.ShapeDtypeStruct((n, width), bf16) for n in sizes],
        scratch_shapes=[
            pltpu.VMEM((rows, width), bf16),
            pltpu.VMEM((rows, width), bf16),
            pltpu.VMEM((rows, 512), bf16),
            pltpu.VMEM((rows, 512), bf16),
            pltpu.SemaphoreType.DMA((4 * len(blocks),)),
            pltpu.SemaphoreType.DMA((4,)),
        ],
        input_output_aliases={first + n: n for n in range(4)} if kept else {},
        compiler_params=pltpu.CompilerParams(vmem_limit_bytes=32 * 2**20),
        cost_estimate=pl.CostEstimate(flops=1, bytes_accessed=1, transcendentals=0),
    )(
        *weights,
        bias_in,
        *[block[0] for block in blocks],
        *[block[1] for block in blocks],
        *(kept or ()),
    )
    return out[:4], out[4], out[5:]


def return_kernel(table, summed, sums, out, buffer):
    buffer[:192, :] = summed[...]
    high = sums[...].astype(bf16).astype(f32)
    low = sums[...] - high
    row = lax.broadcasted_iota(jnp.int32, (16, sums.shape[1]), 0)
    rows = jnp.where(row == 0, high[0:1, :], jnp.where(row == 1, low[0:1, :], 0.0))
    rows = jnp.where(row == 2, high[1:2, :], jnp.where(row == 3, low[1:2, :], rows))
    buffer[192:, :] = rows.astype(bf16)
    out[...] = jnp.dot(table[...], buffer[...], preferred_element_type=f32).astype(bf16)


def return_rows(summed, sums):
    order = np.zeros((16, 16), np.int32)
    order[:, :12] = np.arange(192).reshape(16, 12)
    order[:, 12:] = 192 + np.arange(4)
    table = jnp.asarray(order.reshape(-1, 1) == np.arange(208)[None, :], bf16)
    width = summed.shape[1]
    return pl.pallas_call(
        return_kernel,
        out_shape=jax.ShapeDtypeStruct((256, width), bf16),
        scratch_shapes=[pltpu.VMEM((208, width), bf16)],
        compiler_params=pltpu.CompilerParams(vmem_limit_bytes=24 * 2**20),
    )(table, summed, sums)


def combine_kernel(tok, cot, idx, slot, gain, shift, near, far, out, gain_out, shift_out):
    def summed(ref):
        column = lax.broadcasted_iota(jnp.int32, (8, 256), 1) & 15
        row = lax.broadcasted_iota(jnp.int32, (8, 256), 0)
        table = (column >= 12) & (((column - 12) >> 1) == row)
        return jnp.dot(table.astype(f32).astype(bf16), ref[...], preferred_element_type=f32)

    sums = summed(near) + summed(far)
    shift_out[...] = sums[1:2, :]
    gain_out[...] = (sums[0:1, :] - shift[...] * sums[1:2, :]) / gain[...]
    expert = idx[...]
    core = (expert ^ lax.axis_index("expert")) & 1
    code = jnp.where(slot[...] >= 0, core * 256 + (expert >> 1) * 16 + core * CAP + slot[...], -1000)
    normed_grad = jnp.zeros(tok.shape, f32)
    for part, ref in enumerate((near, far)):
        row = lax.broadcasted_iota(jnp.int32, (256, 128), 0) + part * 256
        table = (code[0:1, :] == row).astype(f32) + (code[1:2, :] == row).astype(f32)
        normed_grad = normed_grad + lax.dot_general(
            table.astype(bf16), ref[...], (((0,), (0,)), ((), ())), preferred_element_type=f32
        )
    standardized, deviation = layer_norm(tok[...])
    scaled = normed_grad * gain[...]
    inner = (
        scaled
        - jnp.mean(scaled, axis=-1, keepdims=True)
        - standardized * jnp.mean(scaled * standardized, axis=-1, keepdims=True)
    )
    out[...] = (cot[...].astype(f32) + deviation * inner).astype(bf16)


def send_order():
    return np.arange(384).reshape(2, 16, 2, CAP).transpose(1, 2, 0, 3).reshape(-1)


def take_order():
    return np.arange(384).reshape(16, 2, 2 * CAP).transpose(1, 0, 2).reshape(-1)


def shards(tokens, cotangent, expert_idx, expert_slot, combine, gain, shift, w_in, b_in, w_out):
    width = tokens.shape[1]
    weight_in, weight_out = w_in[0], w_out[0]
    idx, slot, comb = expert_idx.T, expert_slot.T, combine.T
    gain_row, shift_row = gain.reshape(1, width), shift.reshape(1, width)
    limit = pltpu.CompilerParams(vmem_limit_bytes=24 * 2**20)
    near, far = pl.pallas_call(
        dispatch_kernel,
        out_shape=[jax.ShapeDtypeStruct((192, width), bf16)] * 2,
        scratch_shapes=[pltpu.VMEM((256, width), bf16)],
        compiler_params=limit,
    )(tokens, cotangent, idx, slot, comb, gain_row, shift_row)
    first, second = regroup(send_order(), [near, swapped(far, 1)], [896, 768])
    (own_a,) = regroup(take_order(), [chip_exchange(first)], [896])
    second, _ = lax.optimization_barrier((second, own_a))
    (own_b,) = regroup(take_order(), [chip_exchange(second)], [768])

    l_a, r_a, q_a = right(own_a), left(own_a), across(own_a)
    l_b, r_b, q_b = right(own_b), left(own_b), across(own_b)
    ql_a, f_a, qr_a = right(q_a), left(r_a), across(r_a)
    ql_b, f_b, qr_b = right(q_b), left(r_b), across(r_b)
    qf_a, qf_b = right(ql_a), left(qr_b)

    weight_in, weight_out, _ = lax.optimization_barrier((weight_in, weight_out, own_b))
    step = functools.partial(experts_step, (weight_in, weight_in.T, weight_out.T), b_in)
    early = ((own_a, own_b), (l_a, l_b), (r_a, r_b), (q_a, q_b))
    early, _ = lax.optimization_barrier((early, ql_a))
    kept, bias_a, (p_own, p_l, p_r, p_q) = step(0, early, None, [192] * 4)
    kept, bias_b, (p_ql, p_f, p_qr) = step(
        768, ((ql_a, ql_b), (f_a, f_b), (qr_a, qr_b)), kept, [192] * 3
    )
    kept, bias_c, (low, high) = step(1344, ((qf_a, qf_b),), kept, [96] * 2)
    half = 96
    back_ql, back_qr = left(low), right(high)
    cat = lambda *a: jnp.concatenate(a, axis=0)
    s_ql = cat(add16(p_ql[:half], back_ql), p_ql[half:])
    s_qr = cat(p_qr[:half], add16(p_qr[half:], back_qr))
    p_f, _ = lax.optimization_barrier((p_f, back_qr))
    back_q, back_f, back_r = left(s_ql), right(p_f), across(s_qr)
    s_q = add16(p_q, back_q)
    s_r = add16(p_r, back_f, back_r)
    p_l, _ = lax.optimization_barrier((p_l, back_q))
    summed = add16(p_own, left(p_l), right(s_r), across(s_q))

    over_rows = (((0,), (0,)), ((), ()))
    dot = functools.partial(lax.dot_general, dimension_numbers=over_rows, preferred_element_type=f32)
    inputs, grads, act, grad_pre = kept
    grad_win = lax.optimization_barrier(dot(inputs, grad_pre))
    grad_wout = dot(act, grads)
    grad_bias = bias_a + bias_b + bias_c
    weight_floats = weight_in.astype(f32)
    sums = jnp.stack(
        [jnp.sum(weight_floats * grad_win, axis=1), jnp.sum(weight_floats * grad_bias, axis=1)]
    )
    for mask in (64, 128, 32):
        sums = sums + swapped(sums, mask)

    came = chip_exchange(return_rows(summed, sums))
    came, grad_wout = lax.optimization_barrier((came, grad_wout))
    grad_tokens, gain_gradient, grad_shift = pl.pallas_call(
        combine_kernel,
        out_shape=[jax.ShapeDtypeStruct(tokens.shape, bf16)] + [jax.ShapeDtypeStruct((1, width), f32)] * 2,
        compiler_params=limit,
    )(tokens, cotangent, idx, slot, gain_row, shift_row, came, swapped(came, 1))
    return (
        grad_tokens,
        grad_win[None],
        grad_bias,
        grad_wout[None],
        gain_gradient.reshape(width),
        grad_shift.reshape(width),
    )


def solution(mesh):
    both = P(("dp", "expert"), None)
    return jax.shard_map(
        shards,
        mesh=mesh,
        in_specs=(both,) * 5
        + (P(), P(), P("expert", None, "dp"), P("expert", "dp"), P("expert", "dp", None)),
        out_specs=(both, P("expert", None, "dp"), P("expert", "dp"), P("expert", "dp", None), P(), P()),
        check_vma=False,
    )
```

```python
import functools
import math

import jax
import jax.numpy as jnp
import numpy as np
from jax import lax
from jax.experimental import pallas as pl
from jax.experimental.pallas import tpu as pltpu
from jax.sharding import PartitionSpec as P

inv_root_two = 1.0 / math.sqrt(2.0)
inv_root_tau = 1.0 / math.sqrt(2.0 * math.pi)
f32, bf16 = jnp.float32, jnp.bfloat16

RIGHT = [(i, (i + 2) % 8) for i in range(8)]
LEFT = [(i, (i - 2) % 8) for i in range(8)]
ACROSS = [(i, i ^ 1) for i in range(8)]
CAP = 6
FIRST, SECOND = pl.ds(0, 896), pl.ds(896, 768)


def gelu_parts(value):
    normal_cdf = 0.5 * (1.0 + lax.erf(value * inv_root_two))
    slope = normal_cdf + value * jnp.exp(-0.5 * value * value) * inv_root_tau
    return (value * normal_cdf, slope)


def right(x):
    return lax.ppermute(x, "dp", RIGHT)


def left(x):
    return lax.ppermute(x, "dp", LEFT)


def across(x):
    return lax.ppermute(x, "dp", ACROSS)


def swapped(x, mask):
    return lax.ppermute(x, ("dp", "expert"), [(i, i ^ mask) for i in range(256)])


def add16(*terms):
    total = terms[0].astype(f32)
    for term in terms[1:]:
        total = total + term.astype(f32)
    return total.astype(bf16)


def chip_exchange(x):
    groups = [[2 * n + core for n in range(16)] for core in (0, 1)]
    x = x.reshape(16, x.shape[0] // 16, x.shape[1])
    x = lax.all_to_all(x, "expert", 0, 0, axis_index_groups=groups, tiled=True)
    return x.reshape(-1, x.shape[2])


def layer_norm(tokens):
    floats = tokens.astype(f32)
    centered = floats - jnp.mean(floats, axis=-1, keepdims=True)
    deviation = lax.rsqrt(jnp.mean(centered * centered, axis=-1, keepdims=True) + 1e-06)
    return centered * deviation, deviation


def dispatch_kernel(*refs):
    given, (gain, shift, near, far), (tok, idx, slot, comb, both, sems) = refs[:5], refs[5:9], refs[9:]
    places = (tok, both.at[pl.ds(128, 128)], idx, slot, comb)
    copies = [pltpu.make_async_copy(a, b, sems.at[n]) for n, (a, b) in enumerate(zip(given, places))]
    for copy in copies:
        copy.start()
    for copy in copies:
        copy.wait()
    standardized, _ = layer_norm(tok[...])
    both[:128, :] = (standardized * gain[...].reshape(1, -1) + shift[...].reshape(1, -1)).astype(bf16)
    expert = idx[...]
    core = (expert ^ lax.axis_index("expert")) & 1
    code = jnp.where(slot[...] >= 0, core * 192 + (expert >> 1) * 12 + slot[...], -1000)
    for part, out in enumerate((near, far)):
        row = lax.broadcasted_iota(jnp.int32, (192, 128), 0) + part * 192
        ins = [(code[k : k + 1, :] == row).astype(f32) for k in (0, 1)]
        outs = [(code[k : k + 1, :] + CAP == row).astype(f32) for k in (0, 1)]
        scale = jnp.sum(
            ins[0] + ins[1] + outs[0] * comb[0:1, :] + outs[1] * comb[1:2, :], axis=1, keepdims=True
        )
        table = jnp.concatenate([ins[0] + ins[1], outs[0] + outs[1]], axis=1).astype(bf16)
        picked = jnp.dot(table, both[...], preferred_element_type=f32)
        out[...] = (picked * scale).astype(bf16)


def regroup_kernel(count, table, *refs):
    ins, outs, buffer = refs[:count], refs[count:-1], refs[-1]
    size = ins[0].shape[0]
    for n, ref in enumerate(ins):
        buffer[n * size : (n + 1) * size, :] = ref[...]
    start = 0
    for out in outs:
        columns = out.shape[1]
        out[...] = jnp.dot(
            table[...], buffer[:, start : start + columns], preferred_element_type=f32
        ).astype(bf16)
        start += columns


def regroup(order, pieces, widths):
    rows, width = pieces[0].shape
    whole = rows * len(pieces)
    table = jnp.asarray(order[:, None] == np.arange(whole)[None, :], bf16)
    return pl.pallas_call(
        functools.partial(regroup_kernel, len(pieces)),
        out_shape=[jax.ShapeDtypeStruct((whole, n), bf16) for n in widths],
        scratch_shapes=[pltpu.VMEM((whole, width), bf16)],
        compiler_params=pltpu.CompilerParams(vmem_limit_bytes=24 * 2**20),
        cost_estimate=pl.CostEstimate(flops=1, bytes_accessed=1, transcendentals=0),
    )(table, *pieces)


def experts_kernel(blocks, place, aliased, *refs):
    given, bias_in, refs = refs[:3], refs[3], refs[4:]
    firsts, seconds = refs[:blocks], refs[blocks : 2 * blocks]
    refs = refs[2 * blocks + 4 * aliased :]
    all_in, all_gr, all_act, all_pre, bias = refs[:5]
    partials, scratch = refs[5:-9], refs[-9:]
    weight_in, in_turned, out_turned, inputs, grads, act, grad_pre, sems, out_sems = scratch
    rows = 192 * blocks
    copies = []
    for b in range(blocks):
        r = pl.ds(192 * b, 192)
        for n, (kind, whole) in enumerate(((pl.ds(0, 192), inputs), (pl.ds(192, 192), grads))):
            for m, (part, columns) in enumerate(((firsts[b], FIRST), (seconds[b], SECOND))):
                sem = sems.at[4 * b + 2 * n + m]
                copies.append(pltpu.make_async_copy(part.at[kind], whole.at[r, columns], sem))
    weights = [
        pltpu.make_async_copy(a, b, sems.at[4 * blocks + n])
        for n, (a, b) in enumerate(zip(given, (weight_in, in_turned, out_turned)))
    ]
    weights[0].start()
    for copy in copies:
        copy.start()
    weights[2].start()
    weights[1].start()
    weights[0].wait()
    for copy in copies:
        copy.wait()
    there = pl.ds(place, rows)
    keep = [
        pltpu.make_async_copy(here, out.at[there], out_sems.at[n])
        for n, (here, out) in enumerate(
            [(inputs, all_in), (grads, all_gr), (act, all_act), (grad_pre, all_pre)]
        )
    ]
    keep[0].start()
    keep[1].start()
    pre = jnp.dot(inputs[...], weight_in[...], preferred_element_type=f32) + bias_in[...]
    act_value, slope = gelu_parts(pre)
    act[...] = act_value.astype(bf16)
    keep[2].start()
    weights[2].wait()
    grad = slope * jnp.dot(grads[...], out_turned[...], preferred_element_type=f32)
    bias[...] = jnp.sum(grad, axis=0, keepdims=True)
    grad_pre[...] = grad.astype(bf16)
    keep[3].start()
    weights[1].wait()
    partial = jnp.dot(grad_pre[...], in_turned[...], preferred_element_type=f32).astype(bf16)
    start = 0
    for out in partials:
        out[...] = partial[start : start + out.shape[0], :]
        start += out.shape[0]
    for copy in keep:
        copy.wait()


def experts_step(weights, bias_in, place, blocks, kept, sizes):
    rows = 192 * len(blocks)
    width = weights[0].shape[0]
    vmem, anywhere = pl.BlockSpec(memory_space=pltpu.VMEM), pl.BlockSpec(memory_space=pltpu.HBM)
    first = 4 + 2 * len(blocks)
    out = pl.pallas_call(
        functools.partial(experts_kernel, len(blocks), place, kept is not None),
        in_specs=[anywhere] * 3 + [vmem] + [anywhere] * (2 * len(blocks) + (4 if kept else 0)),
        out_specs=[anywhere] * 4 + [vmem] * (1 + len(sizes)),
        out_shape=[
            jax.ShapeDtypeStruct((1536, width), bf16),
            jax.ShapeDtypeStruct((1536, width), bf16),
            jax.ShapeDtypeStruct((1536, 512), bf16),
            jax.ShapeDtypeStruct((1536, 512), bf16),
            jax.ShapeDtypeStruct((1, 512), f32),
        ]
        + [jax.ShapeDtypeStruct((n, width), bf16) for n in sizes],
        scratch_shapes=[
            pltpu.VMEM((width, 512), bf16),
            pltpu.VMEM((512, width), bf16),
            pltpu.VMEM((width, 512), bf16),
            pltpu.VMEM((rows, width), bf16),
            pltpu.VMEM((rows, width), bf16),
            pltpu.VMEM((rows, 512), bf16),
            pltpu.VMEM((rows, 512), bf16),
            pltpu.SemaphoreType.DMA((4 * len(blocks) + 3,)),
            pltpu.SemaphoreType.DMA((4,)),
        ],
        input_output_aliases={first + n: n for n in range(4)} if kept else {},
        compiler_params=pltpu.CompilerParams(vmem_limit_bytes=60 * 2**20),
        cost_estimate=pl.CostEstimate(flops=1, bytes_accessed=1, transcendentals=0),
    )(
        *weights,
        bias_in,
        *[block[0] for block in blocks],
        *[block[1] for block in blocks],
        *(kept or ()),
    )
    return out[:4], out[4], out[5:]


def return_kernel(table, summed, sums, out, buffer):
    buffer[:192, :] = summed[...]
    high = sums[...].astype(bf16).astype(f32)
    low = sums[...] - high
    row = lax.broadcasted_iota(jnp.int32, (16, sums.shape[1]), 0)
    rows = jnp.where(row == 0, high[0:1, :], jnp.where(row == 1, low[0:1, :], 0.0))
    rows = jnp.where(row == 2, high[1:2, :], jnp.where(row == 3, low[1:2, :], rows))
    buffer[192:, :] = rows.astype(bf16)
    out[...] = jnp.dot(table[...], buffer[...], preferred_element_type=f32).astype(bf16)


def return_rows(summed, sums):
    order = np.zeros((16, 16), np.int32)
    order[:, :12] = np.arange(192).reshape(16, 12)
    order[:, 12:] = 192 + np.arange(4)
    table = jnp.asarray(order.reshape(-1, 1) == np.arange(208)[None, :], bf16)
    width = summed.shape[1]
    return pl.pallas_call(
        return_kernel,
        out_shape=jax.ShapeDtypeStruct((256, width), bf16),
        scratch_shapes=[pltpu.VMEM((208, width), bf16)],
        compiler_params=pltpu.CompilerParams(vmem_limit_bytes=24 * 2**20),
    )(table, summed, sums)


def combine_kernel(tok, cot, idx, slot, gain, shift, near, far, out, gain_out, shift_out):
    def summed(ref):
        column = lax.broadcasted_iota(jnp.int32, (8, 256), 1) & 15
        row = lax.broadcasted_iota(jnp.int32, (8, 256), 0)
        table = (column >= 12) & (((column - 12) >> 1) == row)
        return jnp.dot(table.astype(f32).astype(bf16), ref[...], preferred_element_type=f32)

    sums = summed(near) + summed(far)
    gains = gain[...].reshape(1, -1)
    shift_out[...] = sums[1:2, :].reshape(-1)
    gain_out[...] = ((sums[0:1, :] - shift[...].reshape(1, -1) * sums[1:2, :]) / gains).reshape(-1)
    expert = idx[...]
    core = (expert ^ lax.axis_index("expert")) & 1
    code = jnp.where(slot[...] >= 0, core * 256 + (expert >> 1) * 16 + core * CAP + slot[...], -1000)
    normed_grad = jnp.zeros(tok.shape, f32)
    for part, ref in enumerate((near, far)):
        row = lax.broadcasted_iota(jnp.int32, (256, 128), 0) + part * 256
        table = (code[0:1, :] == row).astype(f32) + (code[1:2, :] == row).astype(f32)
        normed_grad = normed_grad + lax.dot_general(
            table.astype(bf16), ref[...], (((0,), (0,)), ((), ())), preferred_element_type=f32
        )
    standardized, deviation = layer_norm(tok[...])
    scaled = normed_grad * gains
    inner = (
        scaled
        - jnp.mean(scaled, axis=-1, keepdims=True)
        - standardized * jnp.mean(scaled * standardized, axis=-1, keepdims=True)
    )
    out[...] = (cot[...].astype(f32) + deviation * inner).astype(bf16)


def send_order():
    return np.arange(384).reshape(2, 16, 2, CAP).transpose(1, 2, 0, 3).reshape(-1)


def take_order():
    return np.arange(384).reshape(16, 2, 2 * CAP).transpose(1, 0, 2).reshape(-1)


def shards(tokens, cotangent, expert_idx, expert_slot, combine, gain, shift, w_in, b_in, w_out):
    width = tokens.shape[1]
    weight_in, weight_out = w_in[0], w_out[0]
    idx, slot, comb = expert_idx.T, expert_slot.T, combine.T
    gain_row, shift_row = gain, shift
    limit = pltpu.CompilerParams(vmem_limit_bytes=24 * 2**20)
    near, far = pl.pallas_call(
        dispatch_kernel,
        in_specs=[pl.BlockSpec(memory_space=pltpu.HBM)] * 5 + [pl.BlockSpec(memory_space=pltpu.VMEM)] * 2,
        out_shape=[jax.ShapeDtypeStruct((192, width), bf16)] * 2,
        scratch_shapes=[
            pltpu.VMEM((128, width), bf16),
            pltpu.VMEM((2, 128), jnp.int32),
            pltpu.VMEM((2, 128), jnp.int32),
            pltpu.VMEM((2, 128), f32),
            pltpu.VMEM((256, width), bf16),
            pltpu.SemaphoreType.DMA((5,)),
        ],
        compiler_params=pltpu.CompilerParams(vmem_limit_bytes=60 * 2**20),
    )(tokens, cotangent, idx, slot, comb, gain_row, shift_row)
    first, second = regroup(send_order(), [near, swapped(far, 1)], [896, 768])
    (own_a,) = regroup(take_order(), [chip_exchange(first)], [896])
    second, _ = lax.optimization_barrier((second, own_a))
    second = chip_exchange(second)
    in_turned, out_turned, _ = lax.optimization_barrier((weight_in, weight_out, own_a))
    in_turned, out_turned, second = lax.optimization_barrier((in_turned.T, out_turned.T, second))
    (own_b,) = regroup(take_order(), [second], [768])

    l_a, r_a, q_a = right(own_a), left(own_a), across(own_a)
    l_b, r_b, q_b = right(own_b), left(own_b), across(own_b)
    ql_a, f_a, qr_a = right(q_a), left(r_a), across(r_a)
    ql_b, f_b, qr_b = right(q_b), left(r_b), across(r_b)
    qf_a, qf_b = right(ql_a), left(qr_b)

    step = functools.partial(experts_step, (weight_in, in_turned, out_turned), b_in)
    early = ((own_a, own_b), (l_a, l_b), (r_a, r_b), (q_a, q_b))
    early, _ = lax.optimization_barrier((early, ql_a))
    kept, bias_a, (p_own, p_l, p_r, p_q) = step(0, early, None, [192] * 4)
    kept, bias_b, (p_ql, p_f, p_qr) = step(
        768, ((ql_a, ql_b), (f_a, f_b), (qr_a, qr_b)), kept, [192] * 3
    )
    kept, bias_c, (low, high) = step(1344, ((qf_a, qf_b),), kept, [96] * 2)
    half = 96
    back_ql, back_qr = left(low), right(high)
    cat = lambda *a: jnp.concatenate(a, axis=0)
    s_ql = cat(add16(p_ql[:half], back_ql), p_ql[half:])
    s_qr = cat(p_qr[:half], add16(p_qr[half:], back_qr))
    p_f, _ = lax.optimization_barrier((p_f, back_qr))
    back_q, back_f, back_r = left(s_ql), right(p_f), across(s_qr)
    s_q = add16(p_q, back_q)
    s_r = add16(p_r, back_f, back_r)
    p_l, _ = lax.optimization_barrier((p_l, back_q))
    summed = add16(p_own, left(p_l), right(s_r), across(s_q))

    over_rows = (((0,), (0,)), ((), ()))
    dot = functools.partial(lax.dot_general, dimension_numbers=over_rows, preferred_element_type=f32)
    inputs, grads, act, grad_pre = kept
    grad_win = lax.optimization_barrier(dot(inputs, grad_pre))
    grad_wout = dot(act, grads)
    grad_bias = bias_a + bias_b + bias_c
    weight_floats = weight_in.astype(f32)
    sums = jnp.stack(
        [jnp.sum(weight_floats * grad_win, axis=1), jnp.sum(weight_floats * grad_bias, axis=1)]
    )
    for mask in (64, 128, 32):
        sums = sums + swapped(sums, mask)

    came = chip_exchange(return_rows(summed, sums))
    came, grad_wout = lax.optimization_barrier((came, grad_wout))
    grad_tokens, gain_gradient, grad_shift = pl.pallas_call(
        combine_kernel,
        out_shape=[jax.ShapeDtypeStruct(tokens.shape, bf16)] + [jax.ShapeDtypeStruct((width,), f32)] * 2,
        compiler_params=limit,
    )(tokens, cotangent, idx, slot, gain_row, shift_row, came, swapped(came, 1))
    return (
        grad_tokens,
        grad_win[None],
        grad_bias,
        grad_wout[None],
        gain_gradient,
        grad_shift,
    )


def solution(mesh):
    both = P(("dp", "expert"), None)
    return jax.shard_map(
        shards,
        mesh=mesh,
        in_specs=(both,) * 5
        + (P(), P(), P("expert", None, "dp"), P("expert", "dp"), P("expert", "dp", None)),
        out_specs=(both, P("expert", None, "dp"), P("expert", "dp"), P("expert", "dp", None), P(), P()),
        check_vma=False,
    )
```

```python
import functools
import math

import jax
import jax.numpy as jnp
import numpy as np
from jax import lax
from jax.experimental import pallas as pl
from jax.experimental.pallas import tpu as pltpu
from jax.sharding import PartitionSpec as P

inv_root_two = 1.0 / math.sqrt(2.0)
inv_root_tau = 1.0 / math.sqrt(2.0 * math.pi)
f32, bf16 = jnp.float32, jnp.bfloat16

RIGHT = [(i, (i + 2) % 8) for i in range(8)]
LEFT = [(i, (i - 2) % 8) for i in range(8)]
ACROSS = [(i, i ^ 1) for i in range(8)]
CAP = 6
FIRST, SECOND = pl.ds(0, 768), pl.ds(768, 896)


def gelu_parts(value):
    normal_cdf = 0.5 * (1.0 + lax.erf(value * inv_root_two))
    slope = normal_cdf + value * jnp.exp(-0.5 * value * value) * inv_root_tau
    return (value * normal_cdf, slope)


def right(x):
    return lax.ppermute(x, "dp", RIGHT)


def left(x):
    return lax.ppermute(x, "dp", LEFT)


def across(x):
    return lax.ppermute(x, "dp", ACROSS)


def swapped(x, mask):
    return lax.ppermute(x, ("dp", "expert"), [(i, i ^ mask) for i in range(256)])


def add16(*terms):
    total = terms[0].astype(f32)
    for term in terms[1:]:
        total = total + term.astype(f32)
    return total.astype(bf16)


def chip_exchange(x):
    groups = [[2 * n + core for n in range(16)] for core in (0, 1)]
    x = x.reshape(16, x.shape[0] // 16, x.shape[1])
    x = lax.all_to_all(x, "expert", 0, 0, axis_index_groups=groups, tiled=True)
    return x.reshape(-1, x.shape[2])


def layer_norm(tokens):
    floats = tokens.astype(f32)
    centered = floats - jnp.mean(floats, axis=-1, keepdims=True)
    deviation = lax.rsqrt(jnp.mean(centered * centered, axis=-1, keepdims=True) + 1e-06)
    return centered * deviation, deviation


def dispatch_kernel(*refs):
    given, (gain, shift, near, far), (tok, idx, slot, comb, both, sems) = refs[:5], refs[5:9], refs[9:]
    places = (tok, both.at[pl.ds(128, 128)], idx, slot, comb)
    copies = [pltpu.make_async_copy(a, b, sems.at[n]) for n, (a, b) in enumerate(zip(given, places))]
    for copy in copies:
        copy.start()
    for copy in copies:
        copy.wait()
    standardized, _ = layer_norm(tok[...])
    both[:128, :] = (standardized * gain[...].reshape(1, -1) + shift[...].reshape(1, -1)).astype(bf16)
    expert = idx[...]
    core = (expert ^ lax.axis_index("expert")) & 1
    code = jnp.where(slot[...] >= 0, core * 192 + (expert >> 1) * 12 + slot[...], -1000)
    for part, out in enumerate((near, far)):
        row = lax.broadcasted_iota(jnp.int32, (192, 128), 0) + part * 192
        ins = [(code[k : k + 1, :] == row).astype(f32) for k in (0, 1)]
        outs = [(code[k : k + 1, :] + CAP == row).astype(f32) for k in (0, 1)]
        scale = jnp.sum(
            ins[0] + ins[1] + outs[0] * comb[0:1, :] + outs[1] * comb[1:2, :], axis=1, keepdims=True
        )
        table = jnp.concatenate([ins[0] + ins[1], outs[0] + outs[1]], axis=1).astype(bf16)
        picked = jnp.dot(table, both[...], preferred_element_type=f32)
        out[...] = (picked * scale).astype(bf16)


def regroup_kernel(count, table, *refs):
    ins, outs, buffer = refs[:count], refs[count:-1], refs[-1]
    size = ins[0].shape[0]
    for n, ref in enumerate(ins):
        buffer[n * size : (n + 1) * size, :] = ref[...]
    start = 0
    for out in outs:
        columns = out.shape[1]
        out[...] = jnp.dot(
            table[...], buffer[:, start : start + columns], preferred_element_type=f32
        ).astype(bf16)
        start += columns


def regroup(order, pieces, widths):
    rows, width = pieces[0].shape
    whole = rows * len(pieces)
    table = jnp.asarray(order[:, None] == np.arange(whole)[None, :], bf16)
    return pl.pallas_call(
        functools.partial(regroup_kernel, len(pieces)),
        out_shape=[jax.ShapeDtypeStruct((whole, n), bf16) for n in widths],
        scratch_shapes=[pltpu.VMEM((whole, width), bf16)],
        compiler_params=pltpu.CompilerParams(vmem_limit_bytes=24 * 2**20),
        cost_estimate=pl.CostEstimate(flops=1, bytes_accessed=1, transcendentals=0),
    )(table, *pieces)


def experts_kernel(blocks, place, aliased, *refs):
    given, bias_in, refs = refs[:3], refs[3], refs[4:]
    firsts, seconds = refs[:blocks], refs[blocks : 2 * blocks]
    refs = refs[2 * blocks + 4 * aliased :]
    all_in, all_gr, all_act, all_pre, bias, sums = refs[:6]
    partials, scratch = refs[6:-9], refs[-9:]
    weight_in, in_turned, out_turned, inputs, grads, act, grad_pre, sems, out_sems = scratch
    rows = 192 * blocks
    copies = []
    for b in range(blocks):
        r = pl.ds(192 * b, 192)
        for n, (kind, whole) in enumerate(((pl.ds(0, 192), inputs), (pl.ds(192, 192), grads))):
            for m, (part, columns) in enumerate(((firsts[b], FIRST), (seconds[b], SECOND))):
                sem = sems.at[4 * b + 2 * n + m]
                copies.append(pltpu.make_async_copy(part.at[kind], whole.at[r, columns], sem))
    weights = [
        pltpu.make_async_copy(a, b, sems.at[4 * blocks + n])
        for n, (a, b) in enumerate(zip(given, (weight_in, in_turned, out_turned)))
    ]
    weights[0].start()
    for copy in copies:
        copy.start()
    weights[2].start()
    weights[1].start()
    weights[0].wait()
    for copy in copies:
        copy.wait()
    there = pl.ds(place, rows)
    keep = [
        pltpu.make_async_copy(here, out.at[there], out_sems.at[n])
        for n, (here, out) in enumerate(
            [(inputs, all_in), (grads, all_gr), (act, all_act), (grad_pre, all_pre)]
        )
    ]
    keep[0].start()
    keep[1].start()
    pre = jnp.dot(inputs[...], weight_in[...], preferred_element_type=f32) + bias_in[...]
    act_value, slope = gelu_parts(pre)
    act[...] = act_value.astype(bf16)
    keep[2].start()
    weights[2].wait()
    grad = slope * jnp.dot(grads[...], out_turned[...], preferred_element_type=f32)
    bias[...] = jnp.sum(grad, axis=0, keepdims=True)
    grad_pre[...] = grad.astype(bf16)
    keep[3].start()
    weights[1].wait()
    partial = jnp.dot(grad_pre[...], in_turned[...], preferred_element_type=f32)
    sums[0:1, :] = jnp.sum(partial * inputs[...].astype(f32), axis=0, keepdims=True)
    sums[1:2, :] = jnp.sum(partial, axis=0, keepdims=True)
    partial = partial.astype(bf16)
    start = 0
    for out in partials:
        out[...] = partial[start : start + out.shape[0], :]
        start += out.shape[0]
    for copy in keep:
        copy.wait()


def experts_step(weights, bias_in, place, blocks, kept, sizes):
    rows = 192 * len(blocks)
    width = weights[0].shape[0]
    vmem, anywhere = pl.BlockSpec(memory_space=pltpu.VMEM), pl.BlockSpec(memory_space=pltpu.HBM)
    first = 4 + 2 * len(blocks)
    out = pl.pallas_call(
        functools.partial(experts_kernel, len(blocks), place, kept is not None),
        in_specs=[anywhere] * 3 + [vmem] + [anywhere] * (2 * len(blocks) + (4 if kept else 0)),
        out_specs=[anywhere] * 4 + [vmem] * (2 + len(sizes)),
        out_shape=[
            jax.ShapeDtypeStruct((1536, width), bf16),
            jax.ShapeDtypeStruct((1536, width), bf16),
            jax.ShapeDtypeStruct((1536, 512), bf16),
            jax.ShapeDtypeStruct((1536, 512), bf16),
            jax.ShapeDtypeStruct((1, 512), f32),
            jax.ShapeDtypeStruct((2, width), f32),
        ]
        + [jax.ShapeDtypeStruct((n, width), bf16) for n in sizes],
        scratch_shapes=[
            pltpu.VMEM((width, 512), bf16),
            pltpu.VMEM((512, width), bf16),
            pltpu.VMEM((width, 512), bf16),
            pltpu.VMEM((rows, width), bf16),
            pltpu.VMEM((rows, width), bf16),
            pltpu.VMEM((rows, 512), bf16),
            pltpu.VMEM((rows, 512), bf16),
            pltpu.SemaphoreType.DMA((4 * len(blocks) + 3,)),
            pltpu.SemaphoreType.DMA((4,)),
        ],
        input_output_aliases={first + n: n for n in range(4)} if kept else {},
        compiler_params=pltpu.CompilerParams(vmem_limit_bytes=60 * 2**20),
        cost_estimate=pl.CostEstimate(flops=1, bytes_accessed=1, transcendentals=0),
    )(
        *weights,
        bias_in,
        *[block[0] for block in blocks],
        *[block[1] for block in blocks],
        *(kept or ()),
    )
    return out[:4], out[4], out[5], out[6:]


def return_kernel(table, summed, sums, out, buffer):
    buffer[:192, :] = summed[...]
    high = sums[...].astype(bf16).astype(f32)
    low = sums[...] - high
    row = lax.broadcasted_iota(jnp.int32, (16, sums.shape[1]), 0)
    rows = jnp.where(row == 0, high[0:1, :], jnp.where(row == 1, low[0:1, :], 0.0))
    rows = jnp.where(row == 2, high[1:2, :], jnp.where(row == 3, low[1:2, :], rows))
    buffer[192:, :] = rows.astype(bf16)
    out[...] = jnp.dot(table[...], buffer[...], preferred_element_type=f32).astype(bf16)


def return_rows(summed, sums):
    order = np.zeros((16, 16), np.int32)
    order[:, :12] = np.arange(192).reshape(16, 12)
    order[:, 12:] = 192 + np.arange(4)
    table = jnp.asarray(order.reshape(-1, 1) == np.arange(208)[None, :], bf16)
    width = summed.shape[1]
    return pl.pallas_call(
        return_kernel,
        out_shape=jax.ShapeDtypeStruct((256, width), bf16),
        scratch_shapes=[pltpu.VMEM((208, width), bf16)],
        compiler_params=pltpu.CompilerParams(vmem_limit_bytes=24 * 2**20),
    )(table, summed, sums)


def combine_kernel(tok, cot, idx, slot, gain, shift, near, far, out, gain_out, shift_out):
    def summed(ref):
        column = lax.broadcasted_iota(jnp.int32, (8, 256), 1) & 15
        row = lax.broadcasted_iota(jnp.int32, (8, 256), 0)
        table = (column >= 12) & (((column - 12) >> 1) == row)
        return jnp.dot(table.astype(f32).astype(bf16), ref[...], preferred_element_type=f32)

    sums = summed(near) + summed(far)
    gains = gain[...].reshape(1, -1)
    shift_out[...] = sums[1:2, :].reshape(-1)
    gain_out[...] = ((sums[0:1, :] - shift[...].reshape(1, -1) * sums[1:2, :]) / gains).reshape(-1)
    expert = idx[...]
    core = (expert ^ lax.axis_index("expert")) & 1
    code = jnp.where(slot[...] >= 0, core * 256 + (expert >> 1) * 16 + core * CAP + slot[...], -1000)
    normed_grad = jnp.zeros(tok.shape, f32)
    for part, ref in enumerate((near, far)):
        row = lax.broadcasted_iota(jnp.int32, (256, 128), 0) + part * 256
        table = (code[0:1, :] == row).astype(f32) + (code[1:2, :] == row).astype(f32)
        normed_grad = normed_grad + lax.dot_general(
            table.astype(bf16), ref[...], (((0,), (0,)), ((), ())), preferred_element_type=f32
        )
    standardized, deviation = layer_norm(tok[...])
    scaled = normed_grad * gains
    inner = (
        scaled
        - jnp.mean(scaled, axis=-1, keepdims=True)
        - standardized * jnp.mean(scaled * standardized, axis=-1, keepdims=True)
    )
    out[...] = (cot[...].astype(f32) + deviation * inner).astype(bf16)


def send_order():
    return np.arange(384).reshape(2, 16, 2, CAP).transpose(1, 2, 0, 3).reshape(-1)


def take_order():
    return np.arange(384).reshape(16, 2, 2 * CAP).transpose(1, 0, 2).reshape(-1)


def shards(tokens, cotangent, expert_idx, expert_slot, combine, gain, shift, w_in, b_in, w_out):
    width = tokens.shape[1]
    weight_in, weight_out = w_in[0], w_out[0]
    idx, slot, comb = expert_idx.T, expert_slot.T, combine.T
    gain_row, shift_row = gain, shift
    limit = pltpu.CompilerParams(vmem_limit_bytes=24 * 2**20)
    near, far = pl.pallas_call(
        dispatch_kernel,
        in_specs=[pl.BlockSpec(memory_space=pltpu.HBM)] * 5 + [pl.BlockSpec(memory_space=pltpu.VMEM)] * 2,
        out_shape=[jax.ShapeDtypeStruct((192, width), bf16)] * 2,
        scratch_shapes=[
            pltpu.VMEM((128, width), bf16),
            pltpu.VMEM((2, 128), jnp.int32),
            pltpu.VMEM((2, 128), jnp.int32),
            pltpu.VMEM((2, 128), f32),
            pltpu.VMEM((256, width), bf16),
            pltpu.SemaphoreType.DMA((5,)),
        ],
        compiler_params=pltpu.CompilerParams(vmem_limit_bytes=60 * 2**20),
    )(tokens, cotangent, idx, slot, comb, gain_row, shift_row)
    first, second = regroup(send_order(), [near, swapped(far, 1)], [768, 896])
    (own_a,) = regroup(take_order(), [chip_exchange(first)], [768])
    second, _ = lax.optimization_barrier((second, own_a))
    l_a, r_a, q_a = right(own_a), left(own_a), across(own_a)
    ql_a, f_a, qr_a = right(q_a), left(r_a), across(r_a)
    second = chip_exchange(second)
    in_turned, out_turned, _ = lax.optimization_barrier((weight_in, weight_out, own_a))
    in_turned, out_turned, second, *_ = lax.optimization_barrier(
        (in_turned.T, out_turned.T, second, l_a, ql_a, f_a, qr_a)
    )
    (own_b,) = regroup(take_order(), [second], [896])

    l_b, r_b, q_b = right(own_b), left(own_b), across(own_b)
    l_b, r_b, q_b = lax.optimization_barrier((l_b, r_b, q_b))
    ql_b, f_b, qr_b = right(q_b), left(r_b), across(r_b)
    qf_a, qf_b = right(ql_a), left(qr_b)

    step = functools.partial(experts_step, (weight_in, in_turned, out_turned), b_in)
    early = ((own_a, own_b), (l_a, l_b), (r_a, r_b), (q_a, q_b))
    early, _ = lax.optimization_barrier((early, ql_a))
    kept, bias_a, sums_a, (p_own, p_l, p_r, p_q) = step(0, early, None, [192] * 4)
    kept, bias_b, sums_b, (ql_low, ql_high, p_f, qr_low, qr_high) = step(
        768, ((ql_a, ql_b), (f_a, f_b), (qr_a, qr_b)), kept, [96, 96, 192, 96, 96]
    )
    kept, bias_c, sums_c, (low, high) = step(1344, ((qf_a, qf_b),), kept, [96] * 2)
    back_ql, back_qr = left(low), right(high)
    sums = sums_a + sums_b + sums_c
    across_sums = swapped(sums, 32)
    back_qr, across_sums = lax.optimization_barrier((back_qr, across_sums))
    sums = sums + across_sums
    sums = (sums + swapped(sums, 128)) + (swapped(sums, 64) + swapped(sums, 192))
    cat = lambda *a: jnp.concatenate(a, axis=0)
    s_ql = cat(add16(ql_low, back_ql), ql_high)
    s_qr = cat(qr_low, add16(qr_high, back_qr))
    p_f, _ = lax.optimization_barrier((p_f, back_qr))
    back_q, back_f, back_r = left(s_ql), right(p_f), across(s_qr)
    s_q = add16(p_q, back_q)
    s_r = add16(p_r, back_f, back_r)
    p_l, _, _ = lax.optimization_barrier((p_l, s_q, s_r))
    summed = add16(p_own, left(p_l), right(s_r), across(s_q))

    over_rows = (((0,), (0,)), ((), ()))
    dot = functools.partial(lax.dot_general, dimension_numbers=over_rows, preferred_element_type=f32)
    inputs, grads, act, grad_pre = kept
    grad_win = dot(inputs, grad_pre)
    grad_wout = dot(act, grads)
    grad_bias = bias_a + bias_b + bias_c
    summed, grad_win = lax.optimization_barrier((summed, grad_win))
    came = chip_exchange(return_rows(summed, sums))
    came, grad_wout = lax.optimization_barrier((came, grad_wout))
    grad_tokens, gain_gradient, grad_shift = pl.pallas_call(
        combine_kernel,
        out_shape=[jax.ShapeDtypeStruct(tokens.shape, bf16)] + [jax.ShapeDtypeStruct((width,), f32)] * 2,
        compiler_params=limit,
    )(tokens, cotangent, idx, slot, gain_row, shift_row, came, swapped(came, 1))
    return (
        grad_tokens,
        grad_win[None],
        grad_bias,
        grad_wout[None],
        gain_gradient,
        grad_shift,
    )


def solution(mesh):
    both = P(("dp", "expert"), None)
    return jax.shard_map(
        shards,
        mesh=mesh,
        in_specs=(both,) * 5
        + (P(), P(), P("expert", None, "dp"), P("expert", "dp"), P("expert", "dp", None)),
        out_specs=(both, P("expert", None, "dp"), P("expert", "dp"), P("expert", "dp", None), P(), P()),
        check_vma=False,
    )
```

```python
import functools
import math

import jax
import jax.numpy as jnp
import numpy as np
from jax import lax
from jax.experimental import pallas as pl
from jax.experimental.pallas import tpu as pltpu
from jax.sharding import PartitionSpec as P

inv_root_two = 1.0 / math.sqrt(2.0)
inv_root_tau = 1.0 / math.sqrt(2.0 * math.pi)
f32, bf16 = jnp.float32, jnp.bfloat16

RIGHT = [(i, (i + 2) % 8) for i in range(8)]
LEFT = [(i, (i - 2) % 8) for i in range(8)]
ACROSS = [(i, i ^ 1) for i in range(8)]
CAP = 6
FIRST, SECOND = pl.ds(0, 768), pl.ds(768, 896)


def gelu_parts(value):
    normal_cdf = 0.5 * (1.0 + lax.erf(value * inv_root_two))
    slope = normal_cdf + value * jnp.exp(-0.5 * value * value) * inv_root_tau
    return (value * normal_cdf, slope)


def right(x):
    return lax.ppermute(x, "dp", RIGHT)


def left(x):
    return lax.ppermute(x, "dp", LEFT)


def across(x):
    return lax.ppermute(x, "dp", ACROSS)


def swapped(x, mask):
    return lax.ppermute(x, ("dp", "expert"), [(i, i ^ mask) for i in range(256)])


def add16(*terms):
    total = terms[0].astype(f32)
    for term in terms[1:]:
        total = total + term.astype(f32)
    return total.astype(bf16)


def chip_exchange(x):
    groups = [[2 * n + core for n in range(16)] for core in (0, 1)]
    x = x.reshape(16, x.shape[0] // 16, x.shape[1])
    x = lax.all_to_all(x, "expert", 0, 0, axis_index_groups=groups, tiled=True)
    return x.reshape(-1, x.shape[2])


def layer_norm(tokens):
    floats = tokens.astype(f32)
    centered = floats - jnp.mean(floats, axis=-1, keepdims=True)
    deviation = lax.rsqrt(jnp.mean(centered * centered, axis=-1, keepdims=True) + 1e-06)
    return centered * deviation, deviation


def dispatch_kernel(*refs):
    given, (gain, shift, near, far), (tok, idx, slot, comb, both, sems) = refs[:5], refs[5:9], refs[9:]
    places = (tok, both.at[pl.ds(128, 128)], idx, slot, comb)
    copies = [pltpu.make_async_copy(a, b, sems.at[n]) for n, (a, b) in enumerate(zip(given, places))]
    for copy in copies:
        copy.start()
    for copy in copies:
        copy.wait()
    standardized, _ = layer_norm(tok[...])
    both[:128, :] = (standardized * gain[...].reshape(1, -1) + shift[...].reshape(1, -1)).astype(bf16)
    expert = idx[...]
    core = (expert ^ lax.axis_index("expert")) & 1
    code = jnp.where(slot[...] >= 0, core * 192 + (expert >> 1) * 12 + slot[...], -1000)
    for part, out in enumerate((near, far)):
        row = lax.broadcasted_iota(jnp.int32, (192, 128), 0) + part * 192
        ins = [(code[k : k + 1, :] == row).astype(f32) for k in (0, 1)]
        outs = [(code[k : k + 1, :] + CAP == row).astype(f32) for k in (0, 1)]
        scale = jnp.sum(
            ins[0] + ins[1] + outs[0] * comb[0:1, :] + outs[1] * comb[1:2, :], axis=1, keepdims=True
        )
        table = jnp.concatenate([ins[0] + ins[1], outs[0] + outs[1]], axis=1).astype(bf16)
        picked = jnp.dot(table, both[...], preferred_element_type=f32)
        out[...] = (picked * scale).astype(bf16)


def regroup_kernel(count, table, *refs):
    ins, outs, buffer = refs[:count], refs[count:-1], refs[-1]
    size = ins[0].shape[0]
    for n, ref in enumerate(ins):
        buffer[n * size : (n + 1) * size, :] = ref[...]
    start = 0
    for out in outs:
        columns = out.shape[1]
        out[...] = jnp.dot(
            table[...], buffer[:, start : start + columns], preferred_element_type=f32
        ).astype(bf16)
        start += columns


def regroup(order, pieces, widths):
    rows, width = pieces[0].shape
    whole = rows * len(pieces)
    table = jnp.asarray(order[:, None] == np.arange(whole)[None, :], bf16)
    return pl.pallas_call(
        functools.partial(regroup_kernel, len(pieces)),
        out_shape=[jax.ShapeDtypeStruct((whole, n), bf16) for n in widths],
        scratch_shapes=[pltpu.VMEM((whole, width), bf16)],
        compiler_params=pltpu.CompilerParams(vmem_limit_bytes=24 * 2**20),
        cost_estimate=pl.CostEstimate(flops=1, bytes_accessed=1, transcendentals=0),
    )(table, *pieces)


def experts_kernel(blocks, parts, place, aliased, *refs):
    given, bias_in, refs = refs[:3], refs[3], refs[4:]
    whole_blocks = [refs[n * blocks : (n + 1) * blocks] for n in range(parts)]
    refs = refs[parts * blocks + 4 * aliased :]
    all_in, all_gr, all_act, all_pre, bias, sums = refs[:6]
    partials, scratch = refs[6:-9], refs[-9:]
    weight_in, in_turned, out_turned, inputs, grads, act, grad_pre, sems, out_sems = scratch
    rows = 192 * blocks
    copies = []
    for b in range(blocks):
        r = pl.ds(192 * b, 192)
        for n, (kind, whole) in enumerate(((pl.ds(0, 192), inputs), (pl.ds(192, 192), grads))):
            first = whole_blocks[0][b].at[kind]
            second = whole_blocks[1][b].at[kind] if parts == 2 else whole_blocks[1 + n][b]
            for m, (part, columns) in enumerate(((first, FIRST), (second, SECOND))):
                sem = sems.at[4 * b + 2 * n + m]
                copies.append(pltpu.make_async_copy(part, whole.at[r, columns], sem))
    weights = [
        pltpu.make_async_copy(a, b, sems.at[4 * blocks + n])
        for n, (a, b) in enumerate(zip(given, (weight_in, in_turned, out_turned)))
    ]
    weights[0].start()
    for copy in copies:
        copy.start()
    weights[2].start()
    weights[1].start()
    weights[0].wait()
    for copy in copies:
        copy.wait()
    there = pl.ds(place, rows)
    keep = [
        pltpu.make_async_copy(here, out.at[there], out_sems.at[n])
        for n, (here, out) in enumerate(
            [(inputs, all_in), (grads, all_gr), (act, all_act), (grad_pre, all_pre)]
        )
    ]
    keep[0].start()
    keep[1].start()
    pre = jnp.dot(inputs[...], weight_in[...], preferred_element_type=f32) + bias_in[...]
    act_value, slope = gelu_parts(pre)
    act[...] = act_value.astype(bf16)
    keep[2].start()
    weights[2].wait()
    grad = slope * jnp.dot(grads[...], out_turned[...], preferred_element_type=f32)
    bias[...] = jnp.sum(grad, axis=0, keepdims=True)
    grad_pre[...] = grad.astype(bf16)
    keep[3].start()
    weights[1].wait()
    partial = jnp.dot(grad_pre[...], in_turned[...], preferred_element_type=f32)
    sums[0:1, :] = jnp.sum(partial * inputs[...].astype(f32), axis=0, keepdims=True)
    sums[1:2, :] = jnp.sum(partial, axis=0, keepdims=True)
    partial = partial.astype(bf16)
    start = 0
    for out in partials:
        out[...] = partial[start : start + out.shape[0], :]
        start += out.shape[0]
    for copy in keep:
        copy.wait()


def experts_step(weights, bias_in, place, blocks, kept, sizes):
    rows = 192 * len(blocks)
    parts = len(blocks[0])
    width = weights[0].shape[0]
    vmem, anywhere = pl.BlockSpec(memory_space=pltpu.VMEM), pl.BlockSpec(memory_space=pltpu.HBM)
    first = 4 + parts * len(blocks)
    out = pl.pallas_call(
        functools.partial(experts_kernel, len(blocks), parts, place, kept is not None),
        in_specs=[anywhere] * 3 + [vmem] + [anywhere] * (parts * len(blocks) + (4 if kept else 0)),
        out_specs=[anywhere] * 4 + [vmem] * (2 + len(sizes)),
        out_shape=[
            jax.ShapeDtypeStruct((1536, width), bf16),
            jax.ShapeDtypeStruct((1536, width), bf16),
            jax.ShapeDtypeStruct((1536, 512), bf16),
            jax.ShapeDtypeStruct((1536, 512), bf16),
            jax.ShapeDtypeStruct((1, 512), f32),
            jax.ShapeDtypeStruct((2, width), f32),
        ]
        + [jax.ShapeDtypeStruct((n, width), bf16) for n in sizes],
        scratch_shapes=[
            pltpu.VMEM((width, 512), bf16),
            pltpu.VMEM((512, width), bf16),
            pltpu.VMEM((width, 512), bf16),
            pltpu.VMEM((rows, width), bf16),
            pltpu.VMEM((rows, width), bf16),
            pltpu.VMEM((rows, 512), bf16),
            pltpu.VMEM((rows, 512), bf16),
            pltpu.SemaphoreType.DMA((4 * len(blocks) + 3,)),
            pltpu.SemaphoreType.DMA((4,)),
        ],
        input_output_aliases={first + n: n for n in range(4)} if kept else {},
        compiler_params=pltpu.CompilerParams(vmem_limit_bytes=60 * 2**20),
        cost_estimate=pl.CostEstimate(flops=1, bytes_accessed=1, transcendentals=0),
    )(
        *weights,
        bias_in,
        *[block[n] for n in range(parts) for block in blocks],
        *(kept or ()),
    )
    return out[:4], out[4], out[5], out[6:]


def return_kernel(table, summed, sums, out, buffer):
    buffer[:192, :] = summed[...]
    high = sums[...].astype(bf16).astype(f32)
    low = sums[...] - high
    row = lax.broadcasted_iota(jnp.int32, (16, sums.shape[1]), 0)
    rows = jnp.where(row == 0, high[0:1, :], jnp.where(row == 1, low[0:1, :], 0.0))
    rows = jnp.where(row == 2, high[1:2, :], jnp.where(row == 3, low[1:2, :], rows))
    buffer[192:, :] = rows.astype(bf16)
    out[...] = jnp.dot(table[...], buffer[...], preferred_element_type=f32).astype(bf16)


def return_rows(summed, sums):
    order = np.zeros((16, 16), np.int32)
    order[:, :12] = np.arange(192).reshape(16, 12)
    order[:, 12:] = 192 + np.arange(4)
    table = jnp.asarray(order.reshape(-1, 1) == np.arange(208)[None, :], bf16)
    width = summed.shape[1]
    return pl.pallas_call(
        return_kernel,
        out_shape=jax.ShapeDtypeStruct((256, width), bf16),
        scratch_shapes=[pltpu.VMEM((208, width), bf16)],
        compiler_params=pltpu.CompilerParams(vmem_limit_bytes=24 * 2**20),
    )(table, summed, sums)


def combine_kernel(tok, cot, idx, slot, gain, shift, near, far, out, gain_out, shift_out):
    def summed(ref):
        column = lax.broadcasted_iota(jnp.int32, (8, 256), 1) & 15
        row = lax.broadcasted_iota(jnp.int32, (8, 256), 0)
        table = (column >= 12) & (((column - 12) >> 1) == row)
        return jnp.dot(table.astype(f32).astype(bf16), ref[...], preferred_element_type=f32)

    sums = summed(near) + summed(far)
    gains = gain[...].reshape(1, -1)
    shift_out[...] = sums[1:2, :].reshape(-1)
    gain_out[...] = ((sums[0:1, :] - shift[...].reshape(1, -1) * sums[1:2, :]) / gains).reshape(-1)
    expert = idx[...]
    core = (expert ^ lax.axis_index("expert")) & 1
    code = jnp.where(slot[...] >= 0, core * 256 + (expert >> 1) * 16 + core * CAP + slot[...], -1000)
    normed_grad = jnp.zeros(tok.shape, f32)
    for part, ref in enumerate((near, far)):
        row = lax.broadcasted_iota(jnp.int32, (256, 128), 0) + part * 256
        table = (code[0:1, :] == row).astype(f32) + (code[1:2, :] == row).astype(f32)
        normed_grad = normed_grad + lax.dot_general(
            table.astype(bf16), ref[...], (((0,), (0,)), ((), ())), preferred_element_type=f32
        )
    standardized, deviation = layer_norm(tok[...])
    scaled = normed_grad * gains
    inner = (
        scaled
        - jnp.mean(scaled, axis=-1, keepdims=True)
        - standardized * jnp.mean(scaled * standardized, axis=-1, keepdims=True)
    )
    out[...] = (cot[...].astype(f32) + deviation * inner).astype(bf16)


def send_order():
    return np.arange(384).reshape(2, 16, 2, CAP).transpose(1, 2, 0, 3).reshape(-1)


def take_order():
    return np.arange(384).reshape(16, 2, 2 * CAP).transpose(1, 0, 2).reshape(-1)


def shards(tokens, cotangent, expert_idx, expert_slot, combine, gain, shift, w_in, b_in, w_out):
    width = tokens.shape[1]
    weight_in, weight_out = w_in[0], w_out[0]
    idx, slot, comb = expert_idx.T, expert_slot.T, combine.T
    gain_row, shift_row = gain, shift
    limit = pltpu.CompilerParams(vmem_limit_bytes=24 * 2**20)
    near, far = pl.pallas_call(
        dispatch_kernel,
        in_specs=[pl.BlockSpec(memory_space=pltpu.HBM)] * 5 + [pl.BlockSpec(memory_space=pltpu.VMEM)] * 2,
        out_shape=[jax.ShapeDtypeStruct((192, width), bf16)] * 2,
        scratch_shapes=[
            pltpu.VMEM((128, width), bf16),
            pltpu.VMEM((2, 128), jnp.int32),
            pltpu.VMEM((2, 128), jnp.int32),
            pltpu.VMEM((2, 128), f32),
            pltpu.VMEM((256, width), bf16),
            pltpu.SemaphoreType.DMA((5,)),
        ],
        compiler_params=pltpu.CompilerParams(vmem_limit_bytes=60 * 2**20),
    )(tokens, cotangent, idx, slot, comb, gain_row, shift_row)
    first, second = regroup(send_order(), [near, swapped(far, 1)], [768, 896])
    (own_a,) = regroup(take_order(), [chip_exchange(first)], [768])
    l_a, r_a, q_a = right(own_a), left(own_a), across(own_a)
    second, *_ = lax.optimization_barrier((second, l_a, r_a, q_a))
    ql_a, f_a, qr_a = right(q_a), left(r_a), left(q_a)
    qf_a = right(ql_a)
    second = chip_exchange(second)
    in_turned, out_turned, _ = lax.optimization_barrier((weight_in, weight_out, own_a))
    in_turned, out_turned, second, *_ = lax.optimization_barrier(
        (in_turned.T, out_turned.T, second, l_a, qf_a, f_a, qr_a)
    )
    (own_b,) = regroup(take_order(), [second], [896])

    l_b, r_b, q_b = right(own_b), left(own_b), across(own_b)
    l_b, r_b, q_b = lax.optimization_barrier((l_b, r_b, q_b))
    ql_b, f_b, qr_b = right(q_b), left(r_b), across(r_b)

    step = functools.partial(experts_step, (weight_in, in_turned, out_turned), b_in)
    early = ((own_a, own_b), (l_a, l_b), (r_a, r_b), (q_a, q_b))
    early, _ = lax.optimization_barrier((early, ql_a))
    kept, bias_a, sums_a, (p_own, p_l, p_r, p_q) = step(0, early, None, [192] * 4)
    ql_far, qr_far, _ = lax.optimization_barrier((ql_b, qr_b, sums_a))
    qf_b = (right(ql_far[:192]), left(qr_far[192:]))
    kept, bias_b, sums_b, (ql_low, ql_high, p_f, qr_low, qr_high) = step(
        768, ((ql_a, ql_b), (f_a, f_b), (qr_a, qr_b)), kept, [96, 96, 192, 96, 96]
    )
    kept, bias_c, sums_c, (low, high) = step(1344, ((qf_a, *qf_b),), kept, [96] * 2)
    back_ql, back_qr = left(low), right(high)
    sums = sums_a + sums_b + sums_c
    across_sums = swapped(sums, 32)
    back_qr, across_sums = lax.optimization_barrier((back_qr, across_sums))
    sums = sums + across_sums
    sums = (sums + swapped(sums, 128)) + (swapped(sums, 64) + swapped(sums, 192))
    cat = lambda *a: jnp.concatenate(a, axis=0)
    s_ql = cat(add16(ql_low, back_ql), ql_high)
    s_qr = cat(qr_low, add16(qr_high, back_qr))
    p_f, _ = lax.optimization_barrier((p_f, back_qr))
    back_q, back_f, back_r = left(s_ql), right(p_f), across(s_qr)
    s_q = add16(p_q, back_q)
    s_r = add16(p_r, back_f, back_r)
    p_l, _, _ = lax.optimization_barrier((p_l, s_q, s_r))
    summed = add16(p_own, left(p_l), right(s_r), across(s_q))

    over_rows = (((0,), (0,)), ((), ()))
    dot = functools.partial(lax.dot_general, dimension_numbers=over_rows, preferred_element_type=f32)
    inputs, grads, act, grad_pre = kept
    grad_win = dot(inputs, grad_pre)
    grad_wout = dot(act, grads)
    grad_bias = bias_a + bias_b + bias_c
    summed, grad_win = lax.optimization_barrier((summed, grad_win))
    came = chip_exchange(return_rows(summed, sums))
    came, grad_wout = lax.optimization_barrier((came, grad_wout))
    grad_tokens, gain_gradient, grad_shift = pl.pallas_call(
        combine_kernel,
        out_shape=[jax.ShapeDtypeStruct(tokens.shape, bf16)] + [jax.ShapeDtypeStruct((width,), f32)] * 2,
        compiler_params=limit,
    )(tokens, cotangent, idx, slot, gain_row, shift_row, came, swapped(came, 1))
    return (
        grad_tokens,
        grad_win[None],
        grad_bias,
        grad_wout[None],
        gain_gradient,
        grad_shift,
    )


def solution(mesh):
    both = P(("dp", "expert"), None)
    return jax.shard_map(
        shards,
        mesh=mesh,
        in_specs=(both,) * 5
        + (P(), P(), P("expert", None, "dp"), P("expert", "dp"), P("expert", "dp", None)),
        out_specs=(both, P("expert", None, "dp"), P("expert", "dp"), P("expert", "dp", None), P(), P()),
        check_vma=False,
    )
```

```python
import functools
import math

import jax
import jax.numpy as jnp
import numpy as np
from jax import lax
from jax.experimental import pallas as pl
from jax.experimental.pallas import tpu as pltpu
from jax.sharding import PartitionSpec as P

inv_root_two = 1.0 / math.sqrt(2.0)
inv_root_tau = 1.0 / math.sqrt(2.0 * math.pi)
f32, bf16 = jnp.float32, jnp.bfloat16

RIGHT = [(i, (i + 2) % 8) for i in range(8)]
LEFT = [(i, (i - 2) % 8) for i in range(8)]
ACROSS = [(i, i ^ 1) for i in range(8)]
CAP = 6
OVER_LAST = (((1,), (1,)), ((), ()))
FIRST, SECOND = pl.ds(0, 768), pl.ds(768, 896)


def gelu_parts(value):
    normal_cdf = 0.5 * (1.0 + lax.erf(value * inv_root_two))
    slope = normal_cdf + value * jnp.exp(-0.5 * value * value) * inv_root_tau
    return (value * normal_cdf, slope)


def right(x):
    return lax.ppermute(x, "dp", RIGHT)


def left(x):
    return lax.ppermute(x, "dp", LEFT)


def across(x):
    return lax.ppermute(x, "dp", ACROSS)


def swapped(x, mask):
    return lax.ppermute(x, ("dp", "expert"), [(i, i ^ mask) for i in range(256)])


def add16(*terms):
    total = terms[0].astype(f32)
    for term in terms[1:]:
        total = total + term.astype(f32)
    return total.astype(bf16)


def chip_exchange(x):
    groups = [[2 * n + core for n in range(16)] for core in (0, 1)]
    x = x.reshape(16, x.shape[0] // 16, x.shape[1])
    x = lax.all_to_all(x, "expert", 0, 0, axis_index_groups=groups, tiled=True)
    return x.reshape(-1, x.shape[2])


def layer_norm(tokens):
    floats = tokens.astype(f32)
    centered = floats - jnp.mean(floats, axis=-1, keepdims=True)
    deviation = lax.rsqrt(jnp.mean(centered * centered, axis=-1, keepdims=True) + 1e-06)
    return centered * deviation, deviation


def dispatch_kernel(*refs):
    given, (gain, shift, near, far), (tok, idx, slot, comb, both, sems) = refs[:5], refs[5:9], refs[9:]
    places = (tok, both.at[pl.ds(128, 128)], idx, slot, comb)
    copies = [pltpu.make_async_copy(a, b, sems.at[n]) for n, (a, b) in enumerate(zip(given, places))]
    for copy in copies:
        copy.start()
    for copy in copies:
        copy.wait()
    standardized, _ = layer_norm(tok[...])
    both[:128, :] = (standardized * gain[...].reshape(1, -1) + shift[...].reshape(1, -1)).astype(bf16)
    expert = idx[...]
    core = (expert ^ lax.axis_index("expert")) & 1
    code = jnp.where(slot[...] >= 0, core * 192 + (expert >> 1) * 12 + slot[...], -1000)
    for part, out in enumerate((near, far)):
        row = lax.broadcasted_iota(jnp.int32, (192, 128), 0) + part * 192
        ins = [(code[k : k + 1, :] == row).astype(f32) for k in (0, 1)]
        outs = [(code[k : k + 1, :] + CAP == row).astype(f32) for k in (0, 1)]
        scale = jnp.sum(
            ins[0] + ins[1] + outs[0] * comb[0:1, :] + outs[1] * comb[1:2, :], axis=1, keepdims=True
        )
        table = jnp.concatenate([ins[0] + ins[1], outs[0] + outs[1]], axis=1).astype(bf16)
        picked = jnp.dot(table, both[...], preferred_element_type=f32)
        out[...] = (picked * scale).astype(bf16)


def regroup_kernel(count, table, *refs):
    ins, outs, buffer = refs[:count], refs[count:-1], refs[-1]
    size = ins[0].shape[0]
    for n, ref in enumerate(ins):
        buffer[n * size : (n + 1) * size, :] = ref[...]
    start = 0
    for out in outs:
        columns = out.shape[1]
        out[...] = jnp.dot(
            table[...], buffer[:, start : start + columns], preferred_element_type=f32
        ).astype(bf16)
        start += columns


def regroup(order, pieces, widths):
    rows, width = pieces[0].shape
    whole = rows * len(pieces)
    table = jnp.asarray(order[:, None] == np.arange(whole)[None, :], bf16)
    return pl.pallas_call(
        functools.partial(regroup_kernel, len(pieces)),
        out_shape=[jax.ShapeDtypeStruct((whole, n), bf16) for n in widths],
        scratch_shapes=[pltpu.VMEM((whole, width), bf16)],
        compiler_params=pltpu.CompilerParams(vmem_limit_bytes=24 * 2**20),
        cost_estimate=pl.CostEstimate(flops=1, bytes_accessed=1, transcendentals=0),
    )(table, *pieces)


def experts_kernel(blocks, parts, place, aliased, *refs):
    given, bias_in, refs = refs[:2], refs[2], refs[3:]
    whole_blocks = [refs[n * blocks : (n + 1) * blocks] for n in range(parts)]
    refs = refs[parts * blocks + 4 * aliased :]
    all_in, all_gr, all_act, all_pre, bias, sums = refs[:6]
    partials, scratch = refs[6:-8], refs[-8:]
    weight_in, weight_out, inputs, grads, act, grad_pre, sems, out_sems = scratch
    rows = 192 * blocks
    copies = []
    for b in range(blocks):
        r = pl.ds(192 * b, 192)
        for n, (kind, whole) in enumerate(((pl.ds(0, 192), inputs), (pl.ds(192, 192), grads))):
            first = whole_blocks[0][b].at[kind]
            second = whole_blocks[1][b].at[kind] if parts == 2 else whole_blocks[1 + n][b]
            for m, (part, columns) in enumerate(((first, FIRST), (second, SECOND))):
                sem = sems.at[4 * b + 2 * n + m]
                copies.append(pltpu.make_async_copy(part, whole.at[r, columns], sem))
    weights = [
        pltpu.make_async_copy(a, b, sems.at[4 * blocks + n])
        for n, (a, b) in enumerate(zip(given, (weight_in, weight_out)))
    ]
    weights[0].start()
    for copy in copies:
        copy.start()
    weights[1].start()
    weights[0].wait()
    for copy in copies:
        copy.wait()
    there = pl.ds(place, rows)
    keep = [
        pltpu.make_async_copy(here, out.at[there], out_sems.at[n])
        for n, (here, out) in enumerate(
            [(inputs, all_in), (grads, all_gr), (act, all_act), (grad_pre, all_pre)]
        )
    ]
    keep[0].start()
    keep[1].start()
    pre = jnp.dot(inputs[...], weight_in[...], preferred_element_type=f32) + bias_in[...]
    act_value, slope = gelu_parts(pre)
    act[...] = act_value.astype(bf16)
    keep[2].start()
    weights[1].wait()
    grad = slope * lax.dot_general(
        grads[...], weight_out[...], OVER_LAST, preferred_element_type=f32
    )
    bias[...] = jnp.sum(grad, axis=0, keepdims=True)
    grad_pre[...] = grad.astype(bf16)
    keep[3].start()
    partial = lax.dot_general(
        grad_pre[...], weight_in[...], OVER_LAST, preferred_element_type=f32
    )
    sums[0:1, :] = jnp.sum(partial * inputs[...].astype(f32), axis=0, keepdims=True)
    sums[1:2, :] = jnp.sum(partial, axis=0, keepdims=True)
    partial = partial.astype(bf16)
    start = 0
    for out in partials:
        out[...] = partial[start : start + out.shape[0], :]
        start += out.shape[0]
    for copy in keep:
        copy.wait()


def experts_step(weights, bias_in, place, blocks, kept, sizes):
    rows = 192 * len(blocks)
    parts = len(blocks[0])
    width = weights[0].shape[0]
    vmem, anywhere = pl.BlockSpec(memory_space=pltpu.VMEM), pl.BlockSpec(memory_space=pltpu.HBM)
    first = 3 + parts * len(blocks)
    out = pl.pallas_call(
        functools.partial(experts_kernel, len(blocks), parts, place, kept is not None),
        in_specs=[anywhere] * 2 + [vmem] + [anywhere] * (parts * len(blocks) + (4 if kept else 0)),
        out_specs=[anywhere] * 4 + [vmem] * (2 + len(sizes)),
        out_shape=[
            jax.ShapeDtypeStruct((1536, width), bf16),
            jax.ShapeDtypeStruct((1536, width), bf16),
            jax.ShapeDtypeStruct((1536, 512), bf16),
            jax.ShapeDtypeStruct((1536, 512), bf16),
            jax.ShapeDtypeStruct((1, 512), f32),
            jax.ShapeDtypeStruct((2, width), f32),
        ]
        + [jax.ShapeDtypeStruct((n, width), bf16) for n in sizes],
        scratch_shapes=[
            pltpu.VMEM((width, 512), bf16),
            pltpu.VMEM((512, width), bf16),
            pltpu.VMEM((rows, width), bf16),
            pltpu.VMEM((rows, width), bf16),
            pltpu.VMEM((rows, 512), bf16),
            pltpu.VMEM((rows, 512), bf16),
            pltpu.SemaphoreType.DMA((4 * len(blocks) + 3,)),
            pltpu.SemaphoreType.DMA((4,)),
        ],
        input_output_aliases={first + n: n for n in range(4)} if kept else {},
        compiler_params=pltpu.CompilerParams(vmem_limit_bytes=60 * 2**20),
        cost_estimate=pl.CostEstimate(flops=1, bytes_accessed=1, transcendentals=0),
    )(
        *weights,
        bias_in,
        *[block[n] for n in range(parts) for block in blocks],
        *(kept or ()),
    )
    return out[:4], out[4], out[5], out[6:]


def return_kernel(table, summed, sums, out, buffer):
    buffer[:192, :] = summed[...]
    high = sums[...].astype(bf16).astype(f32)
    low = sums[...] - high
    row = lax.broadcasted_iota(jnp.int32, (16, sums.shape[1]), 0)
    rows = jnp.where(row == 0, high[0:1, :], jnp.where(row == 1, low[0:1, :], 0.0))
    rows = jnp.where(row == 2, high[1:2, :], jnp.where(row == 3, low[1:2, :], rows))
    buffer[192:, :] = rows.astype(bf16)
    out[...] = jnp.dot(table[...], buffer[...], preferred_element_type=f32).astype(bf16)


def return_rows(summed, sums):
    order = np.zeros((16, 16), np.int32)
    order[:, :12] = np.arange(192).reshape(16, 12)
    order[:, 12:] = 192 + np.arange(4)
    table = jnp.asarray(order.reshape(-1, 1) == np.arange(208)[None, :], bf16)
    width = summed.shape[1]
    return pl.pallas_call(
        return_kernel,
        out_shape=jax.ShapeDtypeStruct((256, width), bf16),
        scratch_shapes=[pltpu.VMEM((208, width), bf16)],
        compiler_params=pltpu.CompilerParams(vmem_limit_bytes=24 * 2**20),
    )(table, summed, sums)


def combine_kernel(tok, cot, idx, slot, gain, shift, near, far, out, gain_out, shift_out):
    def summed(ref):
        column = lax.broadcasted_iota(jnp.int32, (8, 256), 1) & 15
        row = lax.broadcasted_iota(jnp.int32, (8, 256), 0)
        table = (column >= 12) & (((column - 12) >> 1) == row)
        return jnp.dot(table.astype(f32).astype(bf16), ref[...], preferred_element_type=f32)

    sums = summed(near) + summed(far)
    gains = gain[...].reshape(1, -1)
    shift_out[...] = sums[1:2, :].reshape(-1)
    gain_out[...] = ((sums[0:1, :] - shift[...].reshape(1, -1) * sums[1:2, :]) / gains).reshape(-1)
    expert = idx[...]
    core = (expert ^ lax.axis_index("expert")) & 1
    code = jnp.where(slot[...] >= 0, core * 256 + (expert >> 1) * 16 + core * CAP + slot[...], -1000)
    normed_grad = jnp.zeros(tok.shape, f32)
    for part, ref in enumerate((near, far)):
        row = lax.broadcasted_iota(jnp.int32, (256, 128), 0) + part * 256
        table = (code[0:1, :] == row).astype(f32) + (code[1:2, :] == row).astype(f32)
        normed_grad = normed_grad + lax.dot_general(
            table.astype(bf16), ref[...], (((0,), (0,)), ((), ())), preferred_element_type=f32
        )
    standardized, deviation = layer_norm(tok[...])
    scaled = normed_grad * gains
    inner = (
        scaled
        - jnp.mean(scaled, axis=-1, keepdims=True)
        - standardized * jnp.mean(scaled * standardized, axis=-1, keepdims=True)
    )
    out[...] = (cot[...].astype(f32) + deviation * inner).astype(bf16)


def send_order():
    return np.arange(384).reshape(2, 16, 2, CAP).transpose(1, 2, 0, 3).reshape(-1)


def take_order():
    return np.arange(384).reshape(16, 2, 2 * CAP).transpose(1, 0, 2).reshape(-1)


def shards(tokens, cotangent, expert_idx, expert_slot, combine, gain, shift, w_in, b_in, w_out):
    width = tokens.shape[1]
    weight_in, weight_out = w_in[0], w_out[0]
    idx, slot, comb = expert_idx.T, expert_slot.T, combine.T
    gain_row, shift_row = gain, shift
    limit = pltpu.CompilerParams(vmem_limit_bytes=24 * 2**20)
    near, far = pl.pallas_call(
        dispatch_kernel,
        in_specs=[pl.BlockSpec(memory_space=pltpu.HBM)] * 5 + [pl.BlockSpec(memory_space=pltpu.VMEM)] * 2,
        out_shape=[jax.ShapeDtypeStruct((192, width), bf16)] * 2,
        scratch_shapes=[
            pltpu.VMEM((128, width), bf16),
            pltpu.VMEM((2, 128), jnp.int32),
            pltpu.VMEM((2, 128), jnp.int32),
            pltpu.VMEM((2, 128), f32),
            pltpu.VMEM((256, width), bf16),
            pltpu.SemaphoreType.DMA((5,)),
        ],
        compiler_params=pltpu.CompilerParams(vmem_limit_bytes=60 * 2**20),
    )(tokens, cotangent, idx, slot, comb, gain_row, shift_row)
    (packed,) = regroup(send_order(), [near, swapped(far, 1)], [width])
    own_a, own_b = regroup(take_order(), [chip_exchange(packed)], [768, 896])

    l_a, r_a, q_a = right(own_a), left(own_a), across(own_a)
    l_b, r_b, q_b = right(own_b), left(own_b), across(own_b)
    ql_a, f_a, qr_a = right(q_a), left(r_a), across(r_a)
    ql_b, f_b, qr_b = right(q_b), left(r_b), across(r_b)
    qf_a, qf_b = right(ql_a), left(qr_b)

    step = functools.partial(experts_step, (weight_in, weight_out), b_in)
    early = ((own_a, own_b), (l_a, l_b), (r_a, r_b), (q_a, q_b))
    early, _ = lax.optimization_barrier((early, ql_a))
    kept, bias_a, sums_a, (p_own, p_l, p_r, p_q) = step(0, early, None, [192] * 4)
    kept, bias_b, sums_b, (ql_low, ql_high, p_f, qr_low, qr_high) = step(
        768, ((ql_a, ql_b), (f_a, f_b), (qr_a, qr_b)), kept, [96, 96, 192, 96, 96]
    )
    kept, bias_c, sums_c, (low, high) = step(1344, ((qf_a, qf_b),), kept, [96] * 2)
    back_ql, back_qr = left(low), right(high)
    sums = sums_a + sums_b + sums_c
    across_sums = swapped(sums, 32)
    back_qr, across_sums = lax.optimization_barrier((back_qr, across_sums))
    sums = sums + across_sums
    sums = (sums + swapped(sums, 128)) + (swapped(sums, 64) + swapped(sums, 192))
    cat = lambda *a: jnp.concatenate(a, axis=0)
    s_ql = cat(add16(ql_low, back_ql), ql_high)
    s_qr = cat(qr_low, add16(qr_high, back_qr))
    p_f, _ = lax.optimization_barrier((p_f, back_qr))
    back_q, back_f, back_r = left(s_ql), right(p_f), across(s_qr)
    s_q = add16(p_q, back_q)
    s_r = add16(p_r, back_f, back_r)
    p_l, _, _ = lax.optimization_barrier((p_l, s_q, s_r))
    summed = add16(p_own, left(p_l), right(s_r), across(s_q))

    over_rows = (((0,), (0,)), ((), ()))
    dot = functools.partial(lax.dot_general, dimension_numbers=over_rows, preferred_element_type=f32)
    inputs, grads, act, grad_pre = kept
    grad_win = dot(inputs, grad_pre)
    grad_wout = dot(act, grads)
    grad_bias = bias_a + bias_b + bias_c
    summed, grad_win = lax.optimization_barrier((summed, grad_win))
    came = chip_exchange(return_rows(summed, sums))
    came, grad_wout = lax.optimization_barrier((came, grad_wout))
    grad_tokens, gain_gradient, grad_shift = pl.pallas_call(
        combine_kernel,
        out_shape=[jax.ShapeDtypeStruct(tokens.shape, bf16)] + [jax.ShapeDtypeStruct((width,), f32)] * 2,
        compiler_params=limit,
    )(tokens, cotangent, idx, slot, gain_row, shift_row, came, swapped(came, 1))
    return (
        grad_tokens,
        grad_win[None],
        grad_bias,
        grad_wout[None],
        gain_gradient,
        grad_shift,
    )


def solution(mesh):
    both = P(("dp", "expert"), None)
    return jax.shard_map(
        shards,
        mesh=mesh,
        in_specs=(both,) * 5
        + (P(), P(), P("expert", None, "dp"), P("expert", "dp"), P("expert", "dp", None)),
        out_specs=(both, P("expert", None, "dp"), P("expert", "dp"), P("expert", "dp", None), P(), P()),
        check_vma=False,
    )
```

```python
import functools
import math

import jax
import jax.numpy as jnp
import numpy as np
from jax import lax
from jax.experimental import pallas as pl
from jax.experimental.pallas import tpu as pltpu
from jax.sharding import PartitionSpec as P

inv_root_two = 1.0 / math.sqrt(2.0)
inv_root_tau = 1.0 / math.sqrt(2.0 * math.pi)
f32, bf16 = jnp.float32, jnp.bfloat16

RIGHT = [(i, (i + 2) % 8) for i in range(8)]
LEFT = [(i, (i - 2) % 8) for i in range(8)]
ACROSS = [(i, i ^ 1) for i in range(8)]
CAP = 6
OVER_LAST = (((1,), (1,)), ((), ()))
FIRST, SECOND = pl.ds(0, 768), pl.ds(768, 896)


def gelu_parts(value):
    normal_cdf = 0.5 * (1.0 + lax.erf(value * inv_root_two))
    slope = normal_cdf + value * jnp.exp(-0.5 * value * value) * inv_root_tau
    return (value * normal_cdf, slope)


def right(x):
    return lax.ppermute(x, "dp", RIGHT)


def left(x):
    return lax.ppermute(x, "dp", LEFT)


def across(x):
    return lax.ppermute(x, "dp", ACROSS)


def swapped(x, mask):
    return lax.ppermute(x, ("dp", "expert"), [(i, i ^ mask) for i in range(256)])


def add16(*terms):
    total = terms[0].astype(f32)
    for term in terms[1:]:
        total = total + term.astype(f32)
    return total.astype(bf16)


def chip_exchange(x):
    groups = [[2 * n + core for n in range(16)] for core in (0, 1)]
    x = x.reshape(16, x.shape[0] // 16, x.shape[1])
    x = lax.all_to_all(x, "expert", 0, 0, axis_index_groups=groups, tiled=True)
    return x.reshape(-1, x.shape[2])


def layer_norm(tokens):
    floats = tokens.astype(f32)
    centered = floats - jnp.mean(floats, axis=-1, keepdims=True)
    deviation = lax.rsqrt(jnp.mean(centered * centered, axis=-1, keepdims=True) + 1e-06)
    return centered * deviation, deviation


def dispatch_kernel(*refs):
    given, (gain, shift, near, far), (tok, idx, slot, comb, both, sems) = refs[:5], refs[5:9], refs[9:]
    places = (tok, both.at[pl.ds(128, 128)], idx, slot, comb)
    copies = [pltpu.make_async_copy(a, b, sems.at[n]) for n, (a, b) in enumerate(zip(given, places))]
    for copy in copies:
        copy.start()
    for copy in copies:
        copy.wait()
    standardized, _ = layer_norm(tok[...])
    both[:128, :] = (standardized * gain[...].reshape(1, -1) + shift[...].reshape(1, -1)).astype(bf16)
    expert = idx[...]
    core = (expert ^ lax.axis_index("expert")) & 1
    code = jnp.where(slot[...] >= 0, core * 192 + (expert >> 1) * 12 + slot[...], -1000)
    for part, out in enumerate((near, far)):
        row = lax.broadcasted_iota(jnp.int32, (192, 128), 0) + part * 192
        ins = [(code[k : k + 1, :] == row).astype(f32) for k in (0, 1)]
        outs = [(code[k : k + 1, :] + CAP == row).astype(f32) for k in (0, 1)]
        scale = jnp.sum(
            ins[0] + ins[1] + outs[0] * comb[0:1, :] + outs[1] * comb[1:2, :], axis=1, keepdims=True
        )
        table = jnp.concatenate([ins[0] + ins[1], outs[0] + outs[1]], axis=1).astype(bf16)
        picked = jnp.dot(table, both[...], preferred_element_type=f32)
        out[...] = (picked * scale).astype(bf16)


def regroup_kernel(count, table, *refs):
    ins, outs, buffer = refs[:count], refs[count:-1], refs[-1]
    size = ins[0].shape[0]
    for n, ref in enumerate(ins):
        buffer[n * size : (n + 1) * size, :] = ref[...]
    start = 0
    for out in outs:
        columns = out.shape[1]
        out[...] = jnp.dot(
            table[...], buffer[:, start : start + columns], preferred_element_type=f32
        ).astype(bf16)
        start += columns


def regroup(order, pieces, widths):
    rows, width = pieces[0].shape
    whole = rows * len(pieces)
    table = jnp.asarray(order[:, None] == np.arange(whole)[None, :], bf16)
    return pl.pallas_call(
        functools.partial(regroup_kernel, len(pieces)),
        out_shape=[jax.ShapeDtypeStruct((whole, n), bf16) for n in widths],
        scratch_shapes=[pltpu.VMEM((whole, width), bf16)],
        compiler_params=pltpu.CompilerParams(vmem_limit_bytes=60 * 2**20),
        cost_estimate=pl.CostEstimate(flops=1, bytes_accessed=1, transcendentals=0),
    )(table, *pieces)


def experts_kernel(blocks, parts, place, aliased, *refs):
    given, bias_in, refs = refs[:2], refs[2], refs[3:]
    whole_blocks = [refs[n * blocks : (n + 1) * blocks] for n in range(parts)]
    refs = refs[parts * blocks + 4 * aliased :]
    all_in, all_gr, all_act, all_pre, bias, sums = refs[:6]
    partials, scratch = refs[6:-8], refs[-8:]
    weight_in, weight_out, inputs, grads, act, grad_pre, sems, out_sems = scratch
    rows = 192 * blocks
    copies = []
    for b in range(blocks):
        r = pl.ds(192 * b, 192)
        for n, (kind, whole) in enumerate(((pl.ds(0, 192), inputs), (pl.ds(192, 192), grads))):
            first = whole_blocks[0][b].at[kind]
            second = whole_blocks[1][b].at[kind] if parts == 2 else whole_blocks[1 + n][b]
            for m, (part, columns) in enumerate(((first, FIRST), (second, SECOND))):
                sem = sems.at[4 * b + 2 * n + m]
                copies.append(pltpu.make_async_copy(part, whole.at[r, columns], sem))
    weights = [
        pltpu.make_async_copy(a, b, sems.at[4 * blocks + n])
        for n, (a, b) in enumerate(zip(given, (weight_in, weight_out)))
    ]
    weights[0].start()
    for copy in copies:
        copy.start()
    weights[1].start()
    weights[0].wait()
    for copy in copies:
        copy.wait()
    there = pl.ds(place, rows)
    keep = [
        pltpu.make_async_copy(here, out.at[there], out_sems.at[n])
        for n, (here, out) in enumerate(
            [(inputs, all_in), (grads, all_gr), (act, all_act), (grad_pre, all_pre)]
        )
    ]
    keep[0].start()
    keep[1].start()
    pre = jnp.dot(inputs[...], weight_in[...], preferred_element_type=f32) + bias_in[...]
    act_value, slope = gelu_parts(pre)
    act[...] = act_value.astype(bf16)
    keep[2].start()
    weights[1].wait()
    grad = slope * lax.dot_general(
        grads[...], weight_out[...], OVER_LAST, preferred_element_type=f32
    )
    bias[...] = jnp.sum(grad, axis=0, keepdims=True)
    grad_pre[...] = grad.astype(bf16)
    keep[3].start()
    partial = lax.dot_general(
        grad_pre[...], weight_in[...], OVER_LAST, preferred_element_type=f32
    )
    sums[0:1, :] = jnp.sum(partial * inputs[...].astype(f32), axis=0, keepdims=True)
    sums[1:2, :] = jnp.sum(partial, axis=0, keepdims=True)
    partial = partial.astype(bf16)
    start = 0
    for out in partials:
        out[...] = partial[start : start + out.shape[0], :]
        start += out.shape[0]
    for copy in keep:
        copy.wait()


def experts_step(weights, bias_in, place, blocks, kept, sizes):
    rows = 192 * len(blocks)
    parts = len(blocks[0])
    width = weights[0].shape[0]
    vmem, anywhere = pl.BlockSpec(memory_space=pltpu.VMEM), pl.BlockSpec(memory_space=pltpu.HBM)
    first = 3 + parts * len(blocks)
    out = pl.pallas_call(
        functools.partial(experts_kernel, len(blocks), parts, place, kept is not None),
        in_specs=[anywhere] * 2 + [vmem] + [anywhere] * (parts * len(blocks) + (4 if kept else 0)),
        out_specs=[anywhere] * 4 + [vmem] * (2 + len(sizes)),
        out_shape=[
            jax.ShapeDtypeStruct((1536, width), bf16),
            jax.ShapeDtypeStruct((1536, width), bf16),
            jax.ShapeDtypeStruct((1536, 512), bf16),
            jax.ShapeDtypeStruct((1536, 512), bf16),
            jax.ShapeDtypeStruct((1, 512), f32),
            jax.ShapeDtypeStruct((2, width), f32),
        ]
        + [jax.ShapeDtypeStruct((n, width), bf16) for n in sizes],
        scratch_shapes=[
            pltpu.VMEM((width, 512), bf16),
            pltpu.VMEM((512, width), bf16),
            pltpu.VMEM((rows, width), bf16),
            pltpu.VMEM((rows, width), bf16),
            pltpu.VMEM((rows, 512), bf16),
            pltpu.VMEM((rows, 512), bf16),
            pltpu.SemaphoreType.DMA((4 * len(blocks) + 3,)),
            pltpu.SemaphoreType.DMA((4,)),
        ],
        input_output_aliases={first + n: n for n in range(4)} if kept else {},
        compiler_params=pltpu.CompilerParams(vmem_limit_bytes=60 * 2**20),
        cost_estimate=pl.CostEstimate(flops=1, bytes_accessed=1, transcendentals=0),
    )(
        *weights,
        bias_in,
        *[block[n] for n in range(parts) for block in blocks],
        *(kept or ()),
    )
    return out[:4], out[4], out[5], out[6:]


def return_kernel(table, summed, sums, out, buffer):
    buffer[:192, :] = summed[...]
    high = sums[...].astype(bf16).astype(f32)
    low = sums[...] - high
    row = lax.broadcasted_iota(jnp.int32, (16, sums.shape[1]), 0)
    rows = jnp.where(row == 0, high[0:1, :], jnp.where(row == 1, low[0:1, :], 0.0))
    rows = jnp.where(row == 2, high[1:2, :], jnp.where(row == 3, low[1:2, :], rows))
    buffer[192:, :] = rows.astype(bf16)
    out[...] = jnp.dot(table[...], buffer[...], preferred_element_type=f32).astype(bf16)


def return_rows(summed, sums):
    order = np.zeros((16, 16), np.int32)
    order[:, :12] = np.arange(192).reshape(16, 12)
    order[:, 12:] = 192 + np.arange(4)
    table = jnp.asarray(order.reshape(-1, 1) == np.arange(208)[None, :], bf16)
    width = summed.shape[1]
    return pl.pallas_call(
        return_kernel,
        out_shape=jax.ShapeDtypeStruct((256, width), bf16),
        scratch_shapes=[pltpu.VMEM((208, width), bf16)],
        compiler_params=pltpu.CompilerParams(vmem_limit_bytes=24 * 2**20),
    )(table, summed, sums)


def combine_kernel(tok, cot, idx, slot, gain, shift, near, far, out, gain_out, shift_out):
    def summed(ref):
        column = lax.broadcasted_iota(jnp.int32, (8, 256), 1) & 15
        row = lax.broadcasted_iota(jnp.int32, (8, 256), 0)
        table = (column >= 12) & (((column - 12) >> 1) == row)
        return jnp.dot(table.astype(f32).astype(bf16), ref[...], preferred_element_type=f32)

    sums = summed(near) + summed(far)
    gains = gain[...].reshape(1, -1)
    shift_out[...] = sums[1:2, :].reshape(-1)
    gain_out[...] = ((sums[0:1, :] - shift[...].reshape(1, -1) * sums[1:2, :]) / gains).reshape(-1)
    expert = idx[...]
    core = (expert ^ lax.axis_index("expert")) & 1
    code = jnp.where(slot[...] >= 0, core * 256 + (expert >> 1) * 16 + core * CAP + slot[...], -1000)
    normed_grad = jnp.zeros(tok.shape, f32)
    for part, ref in enumerate((near, far)):
        row = lax.broadcasted_iota(jnp.int32, (256, 128), 0) + part * 256
        table = (code[0:1, :] == row).astype(f32) + (code[1:2, :] == row).astype(f32)
        normed_grad = normed_grad + lax.dot_general(
            table.astype(bf16), ref[...], (((0,), (0,)), ((), ())), preferred_element_type=f32
        )
    standardized, deviation = layer_norm(tok[...])
    scaled = normed_grad * gains
    inner = (
        scaled
        - jnp.mean(scaled, axis=-1, keepdims=True)
        - standardized * jnp.mean(scaled * standardized, axis=-1, keepdims=True)
    )
    out[...] = (cot[...].astype(f32) + deviation * inner).astype(bf16)


def send_order():
    return np.arange(384).reshape(2, 16, 2, CAP).transpose(1, 2, 0, 3).reshape(-1)


def take_order():
    return np.arange(384).reshape(16, 2, 2 * CAP).transpose(1, 0, 2).reshape(-1)


def shards(tokens, cotangent, expert_idx, expert_slot, combine, gain, shift, w_in, b_in, w_out):
    width = tokens.shape[1]
    weight_in, weight_out = w_in[0], w_out[0]
    idx, slot, comb = expert_idx.T, expert_slot.T, combine.T
    gain_row, shift_row = gain, shift
    limit = pltpu.CompilerParams(vmem_limit_bytes=24 * 2**20)
    near, far = pl.pallas_call(
        dispatch_kernel,
        in_specs=[pl.BlockSpec(memory_space=pltpu.HBM)] * 5 + [pl.BlockSpec(memory_space=pltpu.VMEM)] * 2,
        out_shape=[jax.ShapeDtypeStruct((192, width), bf16)] * 2,
        scratch_shapes=[
            pltpu.VMEM((128, width), bf16),
            pltpu.VMEM((2, 128), jnp.int32),
            pltpu.VMEM((2, 128), jnp.int32),
            pltpu.VMEM((2, 128), f32),
            pltpu.VMEM((256, width), bf16),
            pltpu.SemaphoreType.DMA((5,)),
        ],
        compiler_params=pltpu.CompilerParams(vmem_limit_bytes=60 * 2**20),
    )(tokens, cotangent, idx, slot, comb, gain_row, shift_row)
    (packed,) = regroup(send_order(), [near, swapped(far, 1)], [width])
    own_a, own_b = regroup(take_order(), [chip_exchange(packed)], [768, 896])

    l_a, r_a, q_a = right(own_a), left(own_a), across(own_a)
    l_b, r_b, q_b = right(own_b), left(own_b), across(own_b)
    ql_a, f_a, qr_a = right(q_a), left(r_a), across(r_a)
    ql_b, f_b, qr_b = right(q_b), left(r_b), across(r_b)
    qf_a, qf_b = right(ql_a), left(qr_b)

    step = functools.partial(experts_step, (weight_in, weight_out), b_in)
    early = ((own_a, own_b), (l_a, l_b), (r_a, r_b), (q_a, q_b))
    early, _ = lax.optimization_barrier((early, ql_a))
    kept, bias_a, sums_a, (p_own, p_l, p_r, p_q) = step(0, early, None, [192] * 4)
    kept, bias_b, sums_b, (ql_low, ql_high, p_f, qr_low, qr_high) = step(
        768, ((ql_a, ql_b), (f_a, f_b), (qr_a, qr_b)), kept, [96, 96, 192, 96, 96]
    )
    kept, bias_c, sums_c, (low, high) = step(1344, ((qf_a, qf_b),), kept, [96] * 2)
    back_ql, back_qr = left(low), right(high)
    sums = sums_a + sums_b + sums_c
    across_sums = swapped(sums, 32)
    back_qr, across_sums = lax.optimization_barrier((back_qr, across_sums))
    sums = sums + across_sums
    sums = (sums + swapped(sums, 128)) + (swapped(sums, 64) + swapped(sums, 192))
    cat = lambda *a: jnp.concatenate(a, axis=0)
    s_ql = cat(add16(ql_low, back_ql), ql_high)
    s_qr = cat(qr_low, add16(qr_high, back_qr))
    p_f, _ = lax.optimization_barrier((p_f, back_qr))
    back_q, back_f, back_r = left(s_ql), right(p_f), across(s_qr)
    s_q = add16(p_q, back_q)
    s_r = add16(p_r, back_f, back_r)
    p_l, _, _ = lax.optimization_barrier((p_l, s_q, s_r))
    summed = add16(p_own, left(p_l), right(s_r), across(s_q))

    over_rows = (((0,), (0,)), ((), ()))
    dot = functools.partial(lax.dot_general, dimension_numbers=over_rows, preferred_element_type=f32)
    inputs, grads, act, grad_pre = kept
    grad_win = dot(inputs, grad_pre)
    grad_wout = dot(act, grads)
    grad_bias = bias_a + bias_b + bias_c
    summed, grad_win = lax.optimization_barrier((summed, grad_win))
    came = chip_exchange(return_rows(summed, sums))
    came, grad_wout = lax.optimization_barrier((came, grad_wout))
    grad_tokens, gain_gradient, grad_shift = pl.pallas_call(
        combine_kernel,
        out_shape=[jax.ShapeDtypeStruct(tokens.shape, bf16)] + [jax.ShapeDtypeStruct((width,), f32)] * 2,
        compiler_params=limit,
    )(tokens, cotangent, idx, slot, gain_row, shift_row, came, swapped(came, 1))
    return (
        grad_tokens,
        grad_win[None],
        grad_bias,
        grad_wout[None],
        gain_gradient,
        grad_shift,
    )


def solution(mesh):
    both = P(("dp", "expert"), None)
    return jax.shard_map(
        shards,
        mesh=mesh,
        in_specs=(both,) * 5
        + (P(), P(), P("expert", None, "dp"), P("expert", "dp"), P("expert", "dp", None)),
        out_specs=(both, P("expert", None, "dp"), P("expert", "dp"), P("expert", "dp", None), P(), P()),
        check_vma=False,
    )
```
